32 devices in a mesh: groups: 2 (over y), pts: 4 (over z), ffn: 2 (over x), sub: 2 (over core).
Axes of the slice: x: 2, y: 2, z: 4, core: 2. Of those that a mesh axis runs over, the one named last changes fastest.
Arguments:
- points: bfloat16 [32768, 512], P(('groups', 'pts', 'ffn', 'sub')), parts along dimension 0, may hold values from -24 to 24
- part_sizes: int32 [32], P('groups'), parts along dimension 0, may hold values from 1 to 1024, 8192 in all
- norm1_gain: float32 [512], replicated, may hold values from 0.4 to 1.6
- fx_weight: bfloat16 [512, 512], replicated, may hold values from -0.25 to 0.25
- x_weight: bfloat16 [512, 512], replicated, may hold values from -0.25 to 0.25
- slice_weight: bfloat16 [32, 256], replicated, may hold values from -80 to 80
- temp_vector: float32 [32], replicated, may hold values from -1 to 1
- q_weight: bfloat16 [32, 32], replicated, may hold values from -60 to 60
- k_weight: bfloat16 [32, 32], replicated, may hold values from -1 to 1
- v_weight: bfloat16 [32, 32], replicated, may hold values from -1 to 1
- out_weight: bfloat16 [512, 512], replicated, may hold values from -0.25 to 0.25
- norm2_gain: float32 [512], replicated, may hold values from 0.4 to 1.6
- up_weight: bfloat16 [512, 2048], P(None, 'ffn'), may hold values from -0.25 to 0.25
- down_weight: bfloat16 [2048, 512], P('ffn'), may hold values from -0.125 to 0.125
Outputs:
- mixed: bfloat16 [32768, 512], P(('groups', 'pts', 'ffn', 'sub')), parts along dimension 0
The draws below stay inside these ranges and needn't reach their ends.
There are 2 independent parts, one for each index of `groups`. The reference program is written for one: setup_inputs(seed, part) draws one part's arguments, and reference() takes and returns one part's arrays. A program takes and returns all parts, laid end to end along the dimension named above; an argument that names none is the same for every part. Nothing has to cross between parts.
Inputs may be any that keep to these rules, and one draw needn't show every extreme that they name: part_sizes[d] live rows fill the first slots of device d's 1024 slots in the order of pts+ffn+sub; they sum to 8192.
All inputs are finite; a program needn't handle non-finite values.
Results may differ from the reference program's by a relative error of at most 0.007.
The reference program's roundings to bfloat16 on the way count: a program that leaves them out, or rounds other values in their place, can miss the bound.
Values may be sent and summed in bfloat16 or wider, within the bound.
No kernel may reach another device: no remote copies, remote signals or barrier semaphores. Data moves between devices by JAX's collectives and lax.ppermute only.
A program may use at most 64 MiB of HBM per device.

```python
import math
import jax
import jax.numpy as jnp
import numpy as np
from jax import lax

C = 512
H = 16
G = 256
FF = 2048
BAL = 512
DH = 32
NDEV = 16
CAP = 1024


def draw_points(key, part):
    key = jax.random.fold_in(key, 11)
    key_means, key_rough = jax.random.split(key, 2)
    part_means = jax.random.normal(key_means, (NDEV, 1, C), jnp.float32)
    rough_part = jax.random.normal(key_rough, (NDEV, CAP, C), jnp.float32)
    values = 0.8 * part_means + 0.6 * rough_part
    values = jnp.clip(values, -24.0, 24.0)
    return values.reshape(NDEV * CAP, C).astype(jnp.bfloat16)


def draw_slice_weight(key, part):
    key = jax.random.fold_in(key, 23)
    key_entries = jax.random.fold_in(key, 0)
    entries = jax.random.normal(key_entries, (DH, G), jnp.float32) * (3.0 / DH ** 0.5)
    return jnp.clip(entries, -80.0, 80.0).astype(jnp.bfloat16)


def draw_q_weight(key, part):
    key = jax.random.fold_in(key, 37)
    key_entries = jax.random.fold_in(key, 0)
    entries = jax.random.normal(key_entries, (DH, DH), jnp.float32) * (4.0 / DH ** 0.5)
    return jnp.clip(entries, -60.0, 60.0).astype(jnp.bfloat16)


def steps_of(own_key, dims, pieces, smallest, largest):
    loudness = 1.0
    for axis_at, parts in pieces:
        draws = jax.random.uniform(jax.random.fold_in(jax.random.fold_in(own_key, 6), axis_at), (parts,), jnp.float32, smallest / len(pieces), largest / len(pieces))
        loudness = loudness * jnp.repeat(jnp.exp(draws), dims[axis_at] // parts).reshape((-1,) + (1,) * (len(dims) - 1 - axis_at))
    return loudness


def split_up(count, total, reach, lean):
    portions = [(1 << 20) // math.isqrt(standing ** lean) + 1 for standing in range(2, count + 1)]
    surplus, counts = total - reach - (count - 1), [1] * (count - 1)
    while surplus > 0:
        candidates = [i for i in range(count - 1) if counts[i] < reach]
        pool, remaining = sum([portions[i] for i in candidates]), surplus
        for i in candidates:
            more = min(reach - counts[i], max(1, remaining * portions[i] // pool), surplus)
            counts[i] = counts[i] + more
            surplus = surplus - more
    return np.array([reach] + counts)


def ragged_sizes(key, number_of, total, bound, slope):
    if number_of == 2:
        one = jax.random.randint(key, (), max(1, total - bound), min(bound, total - 1) + 1)
        return jnp.stack([one, total - one])
    lengths = jnp.asarray(split_up(number_of, total, bound, slope), jnp.int32)
    pairs = (number_of - 1) // 2
    donor, receiver = lengths[1:1 + 2 * pairs:2], lengths[2:2 + 2 * pairs:2]
    slack = jnp.minimum(donor - 1, bound - receiver)
    moved = jax.random.randint(jax.random.fold_in(key, 1), (pairs,), 0, 1 << 20) % (slack + 1)
    lengths = lengths.at[1:1 + 2 * pairs:2].set(donor - moved).at[2:2 + 2 * pairs:2].set(receiver + moved)
    return lengths[jax.random.permutation(jax.random.fold_in(key, 2), number_of)]


def centred(rng, shape, spread, bound, cuts=(), held_as=jnp.bfloat16):
    values = jax.random.normal(rng, shape, jnp.float32) * spread
    if len(cuts) > 0:
        values = steps_of(rng, shape, cuts, -0.22, 0.18) * values
    return jnp.clip(values, min=-bound, max=bound).astype(held_as)


def setup_inputs(seed: int = 0, part: int = 0) -> dict:
    key_list = jax.random.split(jax.random.key(seed), 15)
    part_keys = jax.random.split(jax.random.fold_in(key_list[14], part), 15)
    return {
        "points": draw_points(jax.random.fold_in(jax.random.fold_in(key_list[14], part), 71), part),
        "part_sizes": ragged_sizes(part_keys[1], NDEV, BAL * NDEV, CAP, 2).astype(jnp.int32),
        "norm1_gain": jnp.clip(1.0 + 0.12 * jax.random.normal(key_list[2], (C,), jnp.float32), 0.4, 1.6),
        "fx_weight": centred(key_list[3], (C, C), C ** -0.5, 0.25),
        "x_weight": centred(key_list[4], (C, C), C ** -0.5, 0.25),
        "slice_weight": draw_slice_weight(jax.random.fold_in(key_list[14], 71), part),
        "temp_vector": centred(key_list[6], (DH,), DH ** -0.5, 1.0, (), jnp.float32),
        "q_weight": draw_q_weight(jax.random.fold_in(key_list[14], 71), part),
        "k_weight": centred(key_list[8], (DH, DH), DH ** -0.5, 1.0),
        "v_weight": centred(key_list[9], (DH, DH), DH ** -0.5, 1.0),
        "out_weight": centred(key_list[10], (C, C), C ** -0.5, 0.25),
        "norm2_gain": jnp.clip(1.0 + 0.12 * jax.random.normal(key_list[11], (C,), jnp.float32), 0.4, 1.6),
        "up_weight": centred(key_list[12], (C, FF), C ** -0.5, 0.25, ((1, 2),)),
        "down_weight": centred(key_list[13], (FF, C), FF ** -0.5, 0.125, ((0, 2),)),
    }


eps_norm = 1e-05
eps_mass = 1e-05
highest_precision = lax.Precision.HIGHEST

def layer_norm(values, gain):
    wide_values = values.astype(jnp.float32)
    centered = wide_values - lax.optimization_barrier(jnp.mean(wide_values, axis=-1, keepdims=True))
    variance = lax.optimization_barrier(jnp.mean(centered * centered, axis=-1, keepdims=True))
    return centered * lax.rsqrt(variance + eps_norm) * gain

def softmax_last(logits):
    shifted = logits - lax.optimization_barrier(jnp.max(logits, axis=-1, keepdims=True))
    raised = jnp.exp(shifted)
    return raised / lax.optimization_barrier(jnp.sum(raised, axis=-1, keepdims=True))

def slice_probs(middles, slice_weight, temp_vector):
    middle_wide = middles.astype(jnp.float32)
    temps = 0.5 + jax.nn.softplus(jnp.einsum('rhd,d->rh', middle_wide, temp_vector, precision=highest_precision))
    logits = jnp.einsum('rhd,dg->rhg', middle_wide, slice_weight.astype(jnp.float32), precision=highest_precision)
    return softmax_last(logits / temps[:, :, None])

def token_mixing(token_sums, weight_sums, q_weight, k_weight, v_weight):
    tokens = (token_sums / (weight_sums[:, :, None] + eps_mass)).astype(jnp.bfloat16).astype(jnp.float32)
    queries = jnp.einsum('hgd,de->hge', tokens, q_weight.astype(jnp.float32), precision=highest_precision)
    keys_all = jnp.einsum('hgd,de->hge', tokens, k_weight.astype(jnp.float32), precision=highest_precision)
    values_all = jnp.einsum('hgd,de->hge', tokens, v_weight.astype(jnp.float32), precision=highest_precision)
    scores = jnp.einsum('hgd,hkd->hgk', queries, keys_all, precision=highest_precision) / math.sqrt(DH)
    probs = softmax_last(scores).astype(jnp.bfloat16).astype(jnp.float32)
    values_narrow = values_all.astype(jnp.bfloat16).astype(jnp.float32)
    mixed_tokens = jnp.einsum('hgk,hkd->hgd', probs, values_narrow, precision=highest_precision)
    return mixed_tokens.astype(jnp.bfloat16)

def reference(points, part_sizes, norm1_gain, fx_weight, x_weight, slice_weight, temp_vector, q_weight, k_weight, v_weight, out_weight, norm2_gain, up_weight, down_weight):
    blocks = points.reshape(NDEV, CAP, C)
    slot_ids = jnp.arange(CAP, dtype=jnp.int32)

    def front(block):
        normed = layer_norm(block, norm1_gain).astype(jnp.bfloat16)
        features = jnp.dot(normed, fx_weight, preferred_element_type=jnp.float32).astype(jnp.bfloat16)
        middles = jnp.dot(normed, x_weight, preferred_element_type=jnp.float32).astype(jnp.bfloat16)
        weights = slice_probs(middles.reshape(CAP, H, DH), slice_weight, temp_vector)
        return (features, weights)

    def accumulate(carry, inputs):
        block, size_here = inputs
        features, weights = front(block)
        live_mask = slot_ids < size_here
        weight_sums, token_sums = carry
        weight_sums = weight_sums + lax.optimization_barrier(jnp.sum(weights * live_mask.astype(jnp.float32)[:, None, None], axis=0))
        masked = weights.astype(jnp.bfloat16) * live_mask.astype(jnp.bfloat16)[:, None, None]
        token_sums = token_sums + jnp.einsum('rhg,rhd->hgd', masked.astype(jnp.float32), features.reshape(CAP, H, DH).astype(jnp.float32), precision=highest_precision)
        return ((weight_sums, token_sums), None)
    start_sums = (jnp.zeros((H, G), jnp.float32), jnp.zeros((H, G, DH), jnp.float32))
    (weight_sums, token_sums), _ = lax.scan(accumulate, start_sums, (blocks, part_sizes))
    mixed_tokens = token_mixing(token_sums, weight_sums, q_weight, k_weight, v_weight).astype(jnp.float32)

    def finish(inputs):
        block, size_here = inputs
        features, weights = front(block)
        narrow = weights.astype(jnp.bfloat16).astype(jnp.float32)
        desliced = jnp.einsum('rhg,hgd->rhd', narrow, mixed_tokens, precision=highest_precision)
        desliced = desliced.astype(jnp.bfloat16).reshape(CAP, C)
        residual = block.astype(jnp.float32) + jnp.dot(desliced, out_weight, preferred_element_type=jnp.float32)
        normed_late = layer_norm(residual, norm2_gain).astype(jnp.bfloat16)
        hidden = jax.nn.gelu(jnp.dot(normed_late, up_weight, preferred_element_type=jnp.float32), approximate=False).astype(jnp.bfloat16)
        update = jnp.dot(hidden, down_weight, preferred_element_type=jnp.float32)
        live_mask = slot_ids < size_here
        return jnp.where(live_mask[:, None], residual + update, 0.0).astype(jnp.bfloat16)
    outputs = lax.map(finish, (blocks, part_sizes))
    return outputs.reshape(NDEV * CAP, C)
```

```python
import functools
import math

import jax
import jax.numpy as jnp
from jax import lax
from jax.experimental import pallas as pl
from jax.experimental.pallas import tpu as pltpu
from jax.sharding import PartitionSpec as P

eps_norm = 1e-05
eps_mass = 1e-05
f32 = jnp.float32
bf16 = jnp.bfloat16
MIB = 1024 * 1024
ROWS = 256


def dot(a, b):
    return jnp.dot(a, b, preferred_element_type=f32)


def layer_norm(wide, gain):
    centered = wide - jnp.mean(wide, axis=-1, keepdims=True)
    variance = jnp.mean(centered * centered, axis=-1, keepdims=True)
    return (centered * lax.rsqrt(variance + eps_norm) * gain).astype(bf16)


def gelu(x):
    z = jnp.clip(x * math.sqrt(0.5), -3.7439211627767994, 3.7439211627767994)
    q = z * z
    num = 0.00022905065861350646
    for c in (
        0.0034082910107109506,
        0.050955695062380861,
        0.18520832239976145,
        1.128379143519084,
    ):
        num = num * q + c
    den = -1.1791602954361697e-7
    for c in (
        0.000023547966471313185,
        0.0010179625278914885,
        0.014070470171167667,
        0.11098505178285362,
        0.49746925110067538,
        1.0,
    ):
        den = den * q + c
    return 0.5 * x * (1.0 + z * num / den)


def front_kernel(
    meta,
    points,
    gain,
    fx_weight,
    x_weight,
    slice_weight,
    temp_vector,
    stored,
    keep,
    send,
    slice_wide,
    temp_wide,
    totals,
):
    heads, head_size, slices = 16, slice_weight.shape[0], slice_weight.shape[1]
    heads = points.shape[1] // head_size
    per_tile = 128 // head_size
    half = heads // 2
    step = pl.program_id(0)

    @pl.when(step == 0)
    def _():
        totals[...] = jnp.zeros_like(totals)
        slice_wide[...] = jnp.zeros_like(slice_wide)
        for j in range(per_tile):
            slice_wide[j, j * head_size : (j + 1) * head_size, :] = slice_weight[...]
        row = lax.broadcasted_iota(jnp.int32, (head_size, head_size), 0)
        col = lax.broadcasted_iota(jnp.int32, (head_size, head_size), 1)
        spread = jnp.where(row == col, jnp.broadcast_to(temp_vector[...], (head_size, head_size)), 0.0)
        column = jnp.sum(spread, axis=1, keepdims=True)
        first = column.astype(bf16).astype(f32)
        second = (column - first).astype(bf16).astype(f32)
        third = column - first - second
        lane = lax.broadcasted_iota(jnp.int32, (head_size, 128), 1)
        for h in range(heads):
            block = jnp.where(lane == h, first, 0.0)
            block = jnp.where(lane == heads + h, second, block)
            block = jnp.where(lane == 2 * heads + h, third, block)
            temp_wide[h * head_size : (h + 1) * head_size, :] = block.astype(bf16)

    @pl.when(step * ROWS < meta[0])
    def _():
        normed = layer_norm(points[...].astype(f32), gain[...])
        features = dot(normed, fx_weight[...])
        middles = dot(normed, x_weight[...]).astype(bf16)
        features_t = features.T.astype(bf16)
        t = dot(middles, temp_wide[...])
        t = t + pltpu.roll(t, 128 - heads, 1) + pltpu.roll(t, 128 - 2 * heads, 1)
        temps = 0.5 + jnp.maximum(t, 0.0) + jnp.log(1.0 + jnp.exp(-jnp.abs(t)))
        scales = math.log2(math.e) / temps
        row = lax.broadcasted_iota(jnp.int32, (ROWS, 1), 0) + step * ROWS
        valid = jnp.where(row < meta[0], 1.0, 0.0)
        for h in range(heads):
            tile = (h // per_tile) * 128
            logits = dot(middles[:, tile : tile + 128], slice_wide[h % per_tile])
            logits = logits * scales[:, h : h + 1]
            top = jnp.max(logits, axis=-1, keepdims=True)
            raised = jnp.exp2(logits - top)
            weights = raised * (valid / jnp.sum(raised, axis=-1, keepdims=True))
            narrow = weights.astype(bf16)
            stored[:, h * slices : (h + 1) * slices] = narrow
            side, at = h // half, h % half
            totals[side, half * head_size + at : half * head_size + at + 1, :] += jnp.sum(
                weights, axis=0, keepdims=True
            )
            totals[side, at * head_size : (at + 1) * head_size, :] += dot(
                features_t[h * head_size : (h + 1) * head_size, :], narrow
            )

    @pl.when(step == pl.num_programs(0) - 1)
    def _():
        keep[...] = totals[meta[1]]
        send[...] = totals[1 - meta[1]]


def mix_kernel(first, second, q_weight, k_weight, v_weight, out):
    head_size = q_weight.shape[0]
    width = first.shape[1]
    half = (first.shape[0]) // (head_size + 1)
    slices = width
    span = half * head_size
    sums = first[...] + second[...]
    parts = []
    for h in range(half):
        mass = sums[span + h : span + h + 1, :] + eps_mass
        parts.append(sums[h * head_size : (h + 1) * head_size, :] / mass)
    tokens = jnp.concatenate(parts, 0).T.astype(bf16)
    total = jnp.zeros((slices, span), f32)
    lane = lax.broadcasted_iota(jnp.int32, (slices, span), 1)
    for h in range(half):
        own = tokens[:, h * head_size : (h + 1) * head_size]
        queries = dot(own, q_weight[...])
        keys = dot(own, k_weight[...])
        values = dot(own, v_weight[...]).astype(bf16)
        scores = lax.dot_general(
            queries,
            keys,
            (((1,), (1,)), ((), ())),
            precision=lax.Precision.HIGHEST,
            preferred_element_type=f32,
        ) / math.sqrt(head_size)
        top = jnp.max(scores, axis=-1, keepdims=True)
        raised = jnp.exp(scores - top)
        probs = (raised / jnp.sum(raised, axis=-1, keepdims=True)).astype(bf16)
        wide = jnp.concatenate([values.astype(f32)] * half, 1)
        wide = jnp.where(lax.div(lane, head_size) == h, wide, 0.0).astype(bf16)
        total = total + dot(probs, wide)
    out[...] = total.astype(bf16)


def back_kernel(
    meta, stored, points, mine, theirs, out_weight, gain, up, down, mixed, spread
):
    slices = mine.shape[0]
    half_width = mine.shape[1]
    width = points.shape[1]
    heads = stored.shape[1] // slices
    head_size = width // heads
    half = heads // 2
    step = pl.program_id(0)
    live = meta[0]

    @pl.when(step == 0)
    def _():
        lane = lax.broadcasted_iota(jnp.int32, (slices, half_width), 1)
        low = meta[1] == 0
        own = mine[...].astype(f32)
        other = theirs[...].astype(f32)
        for side in range(2):
            if side == 0:
                block = jnp.where(low, own, other)
            else:
                block = jnp.where(low, other, own)
            for h in range(half):
                at = (side * half + h) * slices
                spread[at : at + slices, :] = jnp.where(lax.div(lane, head_size) == h, block, 0.0).astype(bf16)

    @pl.when(step * ROWS < live)
    def _():
        middle = half * slices
        left = dot(stored[:, :middle], spread[:middle, :])
        right = dot(stored[:, middle:], spread[middle:, :])
        desliced = jnp.concatenate([left, right], 1).astype(bf16)
        residual = points[...].astype(f32) + dot(desliced, out_weight[...])
        late = layer_norm(residual, gain[...])
        total = residual
        chunk = 512
        for j in range(up.shape[0]):
            for c in range(up.shape[2] // chunk):
                hidden = gelu(dot(late, up[j, :, c * chunk : (c + 1) * chunk])).astype(bf16)
                total = total + dot(hidden, down[j, c * chunk : (c + 1) * chunk, :])
        row = lax.broadcasted_iota(jnp.int32, (ROWS, 1), 0) + step * ROWS
        mixed[...] = jnp.where(row < live, total, 0.0).astype(bf16)

    @pl.when(step * ROWS >= live)
    def _():
        mixed[...] = jnp.zeros_like(mixed)


def whole(shape):
    return pl.BlockSpec(shape, lambda i, m: (0,) * len(shape))


def per_device(
    mesh_shape,
    points,
    part_sizes,
    norm1_gain,
    fx_weight,
    x_weight,
    slice_weight,
    temp_vector,
    q_weight,
    k_weight,
    v_weight,
    out_weight,
    norm2_gain,
    up_weight,
    down_weight,
):
    axes = ("pts", "ffn", "sub")
    devices = math.prod(mesh_shape[a] for a in axes)
    position = lax.axis_index(axes)
    core = lax.axis_index("sub")
    rows, width = points.shape
    head_size, slices = slice_weight.shape
    heads = width // head_size
    half = heads // 2
    live = part_sizes[position]
    meta = jnp.stack([live, core.astype(jnp.int32)])
    steps = rows // ROWS
    up = lax.all_gather(up_weight, "ffn", axis=0)
    down = lax.all_gather(down_weight, "ffn", axis=0)

    sums_rows = half * (head_size + 1)
    last = lambda i, m: jnp.minimum(i, lax.div(m[0] - 1, ROWS))
    stored, keep, send = pl.pallas_call(
        front_kernel,
        grid_spec=pltpu.PrefetchScalarGridSpec(
            num_scalar_prefetch=1,
            grid=(steps,),
            in_specs=[
                pl.BlockSpec((ROWS, width), lambda i, m: (last(i, m), 0)),
                whole((1, width)),
                whole((width, width)),
                whole((width, width)),
                whole((head_size, slices)),
                whole((1, head_size)),
            ],
            out_specs=[
                pl.BlockSpec((ROWS, heads * slices), lambda i, m: (last(i, m), 0)),
                whole((sums_rows, slices)),
                whole((sums_rows, slices)),
            ],
            scratch_shapes=[
                pltpu.VMEM((128 // head_size, 128, slices), bf16),
                pltpu.VMEM((width, 128), bf16),
                pltpu.VMEM((2, sums_rows, slices), f32),
            ],
        ),
        out_shape=[
            jax.ShapeDtypeStruct((rows, heads * slices), bf16),
            jax.ShapeDtypeStruct((sums_rows, slices), f32),
            jax.ShapeDtypeStruct((sums_rows, slices), f32),
        ],
        compiler_params=pltpu.CompilerParams(vmem_limit_bytes=40 * MIB),
        name="front",
    )(
        meta,
        points,
        norm1_gain[None, :],
        fx_weight,
        x_weight,
        slice_weight,
        temp_vector[None, :],
    )

    received = lax.ppermute(send, "sub", [(0, 1), (1, 0)])
    chips = devices // 2
    bits = [2 << b for b in range(chips.bit_length() - 1)]
    turned = bits[1:] + bits[:1]
    sums = keep
    for even, odd in zip(bits, turned):
        sums = sums + received
        received = lax.ppermute(
            sums, axes, [(i, i ^ (odd if i & 1 else even)) for i in range(devices)]
        )
    mine = pl.pallas_call(
        mix_kernel,
        out_shape=jax.ShapeDtypeStruct((slices, half * head_size), bf16),
        compiler_params=pltpu.CompilerParams(vmem_limit_bytes=40 * MIB),
        name="mix",
    )(sums, received, q_weight, k_weight, v_weight)
    theirs = lax.ppermute(mine, "sub", [(0, 1), (1, 0)])

    return pl.pallas_call(
        back_kernel,
        grid_spec=pltpu.PrefetchScalarGridSpec(
            num_scalar_prefetch=1,
            grid=(steps,),
            in_specs=[
                pl.BlockSpec((ROWS, heads * slices), lambda i, m: (last(i, m), 0)),
                pl.BlockSpec((ROWS, width), lambda i, m: (last(i, m), 0)),
                whole(mine.shape),
                whole(mine.shape),
                whole((width, width)),
                whole((1, width)),
                whole(up.shape),
                whole(down.shape),
            ],
            out_specs=pl.BlockSpec((ROWS, width), lambda i, m: (i, 0)),
            scratch_shapes=[pltpu.VMEM((heads * slices, half * head_size), bf16)],
        ),
        out_shape=jax.ShapeDtypeStruct((rows, width), bf16),
        compiler_params=pltpu.CompilerParams(vmem_limit_bytes=48 * MIB),
        name="back",
    )(
        meta,
        stored,
        points,
        mine,
        theirs,
        out_weight,
        norm2_gain[None, :],
        up,
        down,
    )


def solution(mesh):
    return jax.shard_map(
        functools.partial(per_device, dict(mesh.shape)),
        mesh=mesh,
        in_specs=(
            P(("groups", "pts", "ffn", "sub"), None),
            P("groups"),
            P(),
            P(),
            P(),
            P(),
            P(),
            P(),
            P(),
            P(),
            P(),
            P(),
            P(None, "ffn"),
            P("ffn", None),
        ),
        out_specs=P(("groups", "pts", "ffn", "sub"), None),
        check_vma=False,
    )
```

```python
import functools
import math

import jax
import jax.numpy as jnp
from jax import lax
from jax.experimental import pallas as pl
from jax.experimental.pallas import tpu as pltpu
from jax.sharding import PartitionSpec as P

eps_norm = 1e-05
eps_mass = 1e-05
f32 = jnp.float32
bf16 = jnp.bfloat16
MIB = 1024 * 1024
FRONT_ROWS = 256
BACK_ROWS = 512


def dot(a, b):
    return jnp.dot(a, b, preferred_element_type=f32)


def layer_norm(wide, gain):
    centered = wide - jnp.mean(wide, axis=-1, keepdims=True)
    variance = jnp.mean(centered * centered, axis=-1, keepdims=True)
    return (centered * lax.rsqrt(variance + eps_norm) * gain).astype(bf16)


def dot_nt(a, b):
    return lax.dot_general(a, b, (((1,), (1,)), ((), ())), preferred_element_type=f32)


def split3(x):
    first = x.astype(bf16)
    rest = x - first.astype(f32)
    second = rest.astype(bf16)
    third = (rest - second.astype(f32)).astype(bf16)
    return first, second, third


def gelu(x):
    halved = 0.5 * x
    return halved + halved * lax.erf(x * math.sqrt(0.5))


def head_tile(weight, copies):
    size = weight.shape[0]
    wide = jnp.concatenate([weight] * copies, 1)
    tall = jnp.concatenate([wide] * copies, 0)
    row = lax.broadcasted_iota(jnp.int32, tall.shape, 0)
    col = lax.broadcasted_iota(jnp.int32, tall.shape, 1)
    return jnp.where(lax.div(row, size) == lax.div(col, size), tall, 0.0)


def front_kernel(
    sizes,
    place,
    points,
    gain,
    fx_weight,
    x_weight,
    slice_weight,
    temp_vector,
    stored,
    keep,
    send,
    fx_t,
    x_t,
    slice_t,
    temp_t,
    feats,
    mids,
    masses,
    totals,
):
    head_size, slices = slice_weight.shape
    width = points.shape[1]
    heads = width // head_size
    half = heads // 2
    span = half * head_size
    step = pl.program_id(0)
    live = sizes[place[0]]
    core = place[0] % 2

    @pl.when(step == 0)
    def _():
        totals[...] = jnp.zeros_like(totals)
        masses[...] = jnp.zeros_like(masses)
        fx_t[...] = fx_weight[...].astype(f32).T.astype(bf16)
        x_t[...] = x_weight[...].astype(f32).T.astype(bf16)
        slice_t[...] = slice_weight[...].astype(f32).T.astype(bf16)
        wide = jnp.concatenate([temp_vector[...]] * heads, 1)
        row = lax.broadcasted_iota(jnp.int32, (heads, width), 0)
        col = lax.broadcasted_iota(jnp.int32, (heads, width), 1)
        block = jnp.where(lax.div(col, head_size) == row, jnp.broadcast_to(wide, (heads, width)), 0.0)
        for i, part in enumerate(split3(block)):
            temp_t[i * heads : (i + 1) * heads, :] = part

    @pl.when(step * FRONT_ROWS < live)
    def _():
        normed = layer_norm(points[...].astype(f32), gain[...])
        mids[...] = dot_nt(x_t[...], normed).astype(bf16)
        feats[...] = dot_nt(fx_t[...], normed).astype(bf16)
        t = dot(temp_t[...], mids[...])
        t = t[:heads] + t[heads : 2 * heads] + t[2 * heads : 3 * heads]
        temps = 0.5 + jnp.maximum(t, 0.0) + jnp.log(1.0 + jnp.exp(-jnp.abs(t)))
        scales = math.log2(math.e) / temps
        col = lax.broadcasted_iota(jnp.int32, (1, FRONT_ROWS), 1) + step * FRONT_ROWS
        valid = jnp.where(col < live, 1.0, 0.0)
        own = lambda h: slice(h * head_size, (h + 1) * head_size)
        logits = dot(slice_t[...], mids[own(0), :])
        before = None
        for h in range(heads):
            rows = slice(h * slices, (h + 1) * slices)
            ahead = dot(slice_t[...], mids[own(h + 1), :]) if h + 1 < heads else None
            mass, parts = None, []
            for c in range(FRONT_ROWS // 128):
                lanes = slice(c * 128, (c + 1) * 128)
                l = logits[:, lanes]
                top = jnp.max(l, axis=0, keepdims=True)
                raised = jnp.exp2((l - top) * scales[h : h + 1, lanes])
                total = jnp.sum(raised, axis=0, keepdims=True)
                weights = raised * (valid[:, lanes] * pltpu.reciprocal(total, approx=True))
                parts.append(weights.astype(bf16))
                mass = weights if mass is None else mass + weights
            masses[rows, :] += mass
            before = jnp.concatenate(parts, 1)
            stored[rows, :] = before
            logits = ahead
        for h in range(heads):
            side, at = h // half, h % half
            totals[side, at * head_size : (at + 1) * head_size, :] += dot_nt(feats[own(h), :], stored[h * slices : (h + 1) * slices, :])

    @pl.when(step == pl.num_programs(0) - 1)
    def _():
        for h in range(heads):
            mass = jnp.sum(masses[h * slices : (h + 1) * slices, :].T, axis=0, keepdims=True)
            totals[h // half, span + h % half : span + h % half + 1, :] = mass
        keep[...] = totals[core]
        send[...] = totals[1 - core]


def mix_kernel(first, second, q_weight, k_weight, v_weight, out, spread, queries, scores, probs):
    head_size = q_weight.shape[0]
    slices = first.shape[1]
    half = first.shape[0] // (head_size + 1)
    span = half * head_size
    sums = first[...] + second[...]
    parts = []
    for h in range(half):
        mass = sums[span + h : span + h + 1, :] + eps_mass
        parts.append(sums[h * head_size : (h + 1) * head_size, :] / mass)
    tokens_wide = jnp.concatenate(parts, 0).astype(bf16)
    crossed = head_tile(dot_nt(k_weight[...], q_weight[...]), half)
    asked = sum(dot(part, tokens_wide) for part in split3(crossed))
    for i, part in enumerate(split3(asked * (math.log2(math.e) / math.sqrt(head_size)))):
        for h in range(half):
            queries[h, i * head_size : (i + 1) * head_size, :] = part[h * head_size : (h + 1) * head_size, :]
    for h in range(half):
        queries[h, 3 * head_size :, :] = jnp.zeros_like(queries[h, 3 * head_size :, :])
    values = dot(head_tile(v_weight[...].astype(f32), half).T.astype(bf16), tokens_wide).astype(bf16)
    row = lax.broadcasted_iota(jnp.int32, (span, half * 128), 0)
    col = lax.broadcasted_iota(jnp.int32, (span, half * 128), 1)
    same = (lax.div(row, head_size) == lax.div(col, 128)) & (lax.rem(row, head_size) == lax.rem(col, head_size))
    repeat = jnp.where(same, 1.0, 0.0).astype(bf16)
    tokens = tokens_wide.astype(f32).T.astype(bf16)
    spread[...] = dot(tokens, repeat).astype(bf16)
    for h in range(half):
        scores[h] = dot(spread[:, h * 128 : (h + 1) * 128], queries[h])
    for h in range(half):
        top = jnp.max(scores[h], axis=0, keepdims=True)
        raised = jnp.exp2(scores[h] - top)
        total = jnp.sum(raised, axis=0, keepdims=True)
        probs[h] = (raised * pltpu.reciprocal(total, approx=True)).astype(bf16)
    for h in range(half):
        own = slice(h * head_size, (h + 1) * head_size)
        out[own, :] = dot(values[own, :], probs[h]).astype(bf16)


def back_kernel(sizes, place, stored, points, mine, theirs, out_weight, gain, up, down, *refs):
    extra = len(refs) - 6
    sent, (mixed, spread, desliced, ups, downs, arrived) = refs[:extra], refs[extra:]
    span, slices = mine.shape
    width = points.shape[1]
    heads = stored.shape[0] // slices
    head_size = width // heads
    piece = ups.shape[2]
    step = pl.program_id(0)
    live = sizes[place[0]]
    low = place[0] % 2 == 0

    sources = [
        (up.at[:, pl.ds(c * piece, piece)], down.at[pl.ds(c * piece, piece), :]) for c in range(2)
    ]
    if piece == width:
        sources += [(r.at[pl.ds(0, width), :], r.at[pl.ds(width, piece), :]) for r in sent]
    else:
        sources += [(sent[2 * i], sent[2 * i + 1]) for i in range(extra // 2)]

    def copies(n):
        return (
            pltpu.make_async_copy(sources[n][0], ups.at[n], arrived.at[2 * n]),
            pltpu.make_async_copy(sources[n][1], downs.at[n], arrived.at[2 * n + 1]),
        )

    @pl.when(step == 0)
    def _():
        for n in range(len(sources)):
            for copy in copies(n):
                copy.start()
        own = mine[...].astype(f32)
        other = theirs[...].astype(f32)
        spread[:span, :] = jnp.where(low, own, other).astype(bf16)
        spread[span:, :] = jnp.where(low, other, own).astype(bf16)

    @pl.when(step * BACK_ROWS < live)
    def _():
        for h in range(heads):
            own = slice(h * head_size, (h + 1) * head_size)
            desliced[own, :] = dot(spread[own, :], stored[h * slices : (h + 1) * slices, :])
        picked = desliced[...].T.astype(bf16)
        residual = points[...].astype(f32) + dot(picked, out_weight[...])
        late = layer_norm(residual, gain[...])
        total = residual

        @pl.when(step == 0)
        def _():
            for n in range(len(sources)):
                for copy in copies(n):
                    copy.wait()

        raw = dot(late, ups[0])
        for n in range(len(sources)):
            now = raw
            if n + 1 < len(sources):
                raw = dot(late, ups[n + 1])
            total = total + dot(gelu(now).astype(bf16), downs[n])
        row = lax.broadcasted_iota(jnp.int32, (BACK_ROWS, 1), 0) + step * BACK_ROWS
        mixed[...] = jnp.where(row < live, total, 0.0).astype(bf16)

    @pl.when(step * BACK_ROWS >= live)
    def _():
        mixed[...] = jnp.zeros_like(mixed)


def whole(shape):
    return pl.BlockSpec(shape, lambda i, s, p: (0,) * len(shape))


def front_call(sizes, place, points, gain, fx_weight, x_weight, slice_weight, temp_vector):
    rows, width = points.shape
    head_size, slices = slice_weight.shape
    heads = width // head_size
    sums_rows = heads // 2 * (head_size + 1)
    last = lambda i, s, p: jnp.minimum(i, lax.div(s[p[0]] - 1, FRONT_ROWS))
    return pl.pallas_call(
        front_kernel,
        grid_spec=pltpu.PrefetchScalarGridSpec(
            num_scalar_prefetch=2,
            grid=(rows // FRONT_ROWS,),
            in_specs=[
                pl.BlockSpec((FRONT_ROWS, width), lambda i, s, p: (last(i, s, p), 0)),
                whole((1, width)),
                whole((width, width)),
                whole((width, width)),
                whole((head_size, slices)),
                whole((1, head_size)),
            ],
            out_specs=[
                pl.BlockSpec((heads * slices, FRONT_ROWS), lambda i, s, p: (0, last(i, s, p))),
                whole((sums_rows, slices)),
                whole((sums_rows, slices)),
            ],
            scratch_shapes=[
                pltpu.VMEM((width, width), bf16),
                pltpu.VMEM((width, width), bf16),
                pltpu.VMEM((slices, head_size), bf16),
                pltpu.VMEM((3 * heads, width), bf16),
                pltpu.VMEM((width, FRONT_ROWS), bf16),
                pltpu.VMEM((width, FRONT_ROWS), bf16),
                pltpu.VMEM((heads * slices, 128), f32),
                pltpu.VMEM((2, sums_rows, slices), f32),
            ],
        ),
        out_shape=[
            jax.ShapeDtypeStruct((heads * slices, rows), bf16),
            jax.ShapeDtypeStruct((sums_rows, slices), f32),
            jax.ShapeDtypeStruct((sums_rows, slices), f32),
        ],
        compiler_params=pltpu.CompilerParams(vmem_limit_bytes=60 * MIB),
        name="front",
    )(
        sizes,
        place,
        points,
        gain[None, :],
        fx_weight,
        x_weight,
        slice_weight,
        temp_vector[None, :],
    )


def mix_call(first, second, q_weight, k_weight, v_weight):
    head_size = q_weight.shape[0]
    slices = first.shape[1]
    half = first.shape[0] // (head_size + 1)
    return pl.pallas_call(
        mix_kernel,
        out_shape=jax.ShapeDtypeStruct((half * head_size, slices), bf16),
        scratch_shapes=[
            pltpu.VMEM((slices, half * 128), bf16),
            pltpu.VMEM((half, 128, slices), bf16),
            pltpu.VMEM((half, slices, slices), f32),
            pltpu.VMEM((half, slices, slices), bf16),
        ],
        compiler_params=pltpu.CompilerParams(vmem_limit_bytes=60 * MIB),
        name="mix",
    )(first, second, q_weight, k_weight, v_weight)


def back_call(sizes, place, stored, points, mine, theirs, out_weight, gain, up, down, sent):
    rows, width = points.shape
    tall = stored.shape[0]
    piece = up.shape[1] // 2
    pieces = 2 + (len(sent) if piece == width else len(sent) // 2)
    last = lambda i, s, p: jnp.minimum(i, lax.div(s[p[0]] - 1, BACK_ROWS))
    return pl.pallas_call(
        back_kernel,
        grid_spec=pltpu.PrefetchScalarGridSpec(
            num_scalar_prefetch=2,
            grid=(rows // BACK_ROWS,),
            in_specs=[
                pl.BlockSpec((tall, BACK_ROWS), lambda i, s, p: (0, last(i, s, p))),
                pl.BlockSpec((BACK_ROWS, width), lambda i, s, p: (last(i, s, p), 0)),
                whole(mine.shape),
                whole(mine.shape),
                whole((width, width)),
                whole((1, width)),
            ]
            + [pl.BlockSpec(memory_space=pl.ANY)] * (2 + len(sent)),
            out_specs=pl.BlockSpec((BACK_ROWS, width), lambda i, s, p: (i, 0)),
            scratch_shapes=[
                pltpu.VMEM((width, mine.shape[1]), bf16),
                pltpu.VMEM((width, BACK_ROWS), f32),
                pltpu.VMEM((pieces, width, piece), bf16),
                pltpu.VMEM((pieces, piece, width), bf16),
                pltpu.SemaphoreType.DMA((2 * pieces,)),
            ],
        ),
        out_shape=jax.ShapeDtypeStruct((rows, width), bf16),
        compiler_params=pltpu.CompilerParams(vmem_limit_bytes=60 * MIB),
        name="back",
    )(sizes, place, stored, points, mine, theirs, out_weight, gain[None, :], up, down, *sent)


def per_device(
    mesh_shape,
    points,
    part_sizes,
    norm1_gain,
    fx_weight,
    x_weight,
    slice_weight,
    temp_vector,
    q_weight,
    k_weight,
    v_weight,
    out_weight,
    norm2_gain,
    up_weight,
    down_weight,
):
    axes = ("pts", "ffn", "sub")
    devices = math.prod(mesh_shape[a] for a in axes)
    shards = mesh_shape["ffn"]
    place = lax.axis_index(axes).astype(jnp.int32).reshape(1)

    piece = up_weight.shape[1] // 2
    core = lax.axis_index("sub")
    halves = (
        lax.dynamic_slice_in_dim(up_weight, core * piece, piece, 1),
        lax.dynamic_slice_in_dim(down_weight, core * piece, piece, 0),
    )
    if piece == up_weight.shape[0]:
        halves = (jnp.concatenate(halves, 0),)
    far_pieces = [
        lax.ppermute(half, "ffn", [(i, (i + turn) % shards) for i in range(shards)])
        for turn in range(1, shards)
        for half in halves
    ]
    stored, keep, send = front_call(
        part_sizes, place, points, norm1_gain, fx_weight, x_weight, slice_weight, temp_vector
    )
    received = lax.ppermute(send, "sub", [(0, 1), (1, 0)])
    bits = [2 << b for b in range((devices // 2).bit_length() - 1)]
    sums = keep
    hops = None
    for even, odd in zip(bits, bits[1:] + bits[:1]):
        sums = sums + received
        if even == bits[2]:
            ready = lax.optimization_barrier((tuple(far_pieces), sums))[0]
            hops = [lax.ppermute(piece, "sub", [(0, 1), (1, 0)]) for piece in ready]
        received = lax.ppermute(
            sums, axes, [(i, i ^ (odd if i & 1 else even)) for i in range(devices)]
        )
    mine = mix_call(sums, received, q_weight, k_weight, v_weight)
    theirs = lax.ppermute(mine, "sub", [(0, 1), (1, 0)])
    return back_call(
        part_sizes,
        place,
        stored,
        points,
        mine,
        theirs,
        out_weight,
        norm2_gain,
        up_weight,
        down_weight,
        far_pieces + hops,
    )


def solution(mesh):
    return jax.shard_map(
        functools.partial(per_device, dict(mesh.shape)),
        mesh=mesh,
        in_specs=(
            P(("groups", "pts", "ffn", "sub"), None),
            P("groups"),
            P(),
            P(),
            P(),
            P(),
            P(),
            P(),
            P(),
            P(),
            P(),
            P(),
            P(None, "ffn"),
            P("ffn", None),
        ),
        out_specs=P(("groups", "pts", "ffn", "sub"), None),
        check_vma=False,
    )
```

```python
import functools
import math

import jax
import jax.numpy as jnp
from jax import lax
from jax.experimental import pallas as pl
from jax.experimental.pallas import tpu as pltpu
from jax.sharding import PartitionSpec as P

eps_norm = 1e-05
eps_mass = 1e-05
f32 = jnp.float32
bf16 = jnp.bfloat16
MIB = 1024 * 1024
FRONT_ROWS = 512
BACK_ROWS = 512


def dot(a, b):
    return jnp.dot(a, b, preferred_element_type=f32)


def dot_nt(a, b):
    return lax.dot_general(a, b, (((1,), (1,)), ((), ())), preferred_element_type=f32)


def split3(x):
    first = x.astype(bf16)
    rest = x - first.astype(f32)
    second = rest.astype(bf16)
    third = (rest - second.astype(f32)).astype(bf16)
    return first, second, third


def layer_norm(wide, gain):
    centered = wide - jnp.mean(wide, axis=-1, keepdims=True)
    variance = jnp.mean(centered * centered, axis=-1, keepdims=True)
    return (centered * lax.rsqrt(variance + eps_norm) * gain).astype(bf16)


def gelu(x):
    halved = 0.5 * x
    return halved + halved * lax.erf(x * math.sqrt(0.5))


def head_tile(weight, copies):
    size = weight.shape[0]
    wide = jnp.concatenate([weight] * copies, 1)
    tall = jnp.concatenate([wide] * copies, 0)
    row = lax.broadcasted_iota(jnp.int32, tall.shape, 0)
    col = lax.broadcasted_iota(jnp.int32, tall.shape, 1)
    return jnp.where(lax.div(row, size) == lax.div(col, size), tall, 0.0)


def front_kernel(
    sizes,
    place,
    gain,
    slice_weight,
    temp_vector,
    points,
    fx_weight,
    x_weight,
    stored,
    keep,
    send,
    fx_t,
    x_t,
    slice_t,
    temp_t,
    feats,
    mids,
    totals,
):
    head_size, slices = slice_weight.shape
    width = points.shape[1]
    heads = width // head_size
    half = heads // 2
    span = half * head_size
    live = sizes[place[0]]
    core = place[0] % 2
    totals[...] = jnp.zeros_like(totals)
    slice_t[...] = slice_weight[...].astype(f32).T.astype(bf16)
    wide = jnp.concatenate([temp_vector[...]] * heads, 1)
    row = lax.broadcasted_iota(jnp.int32, (heads, width), 0)
    col = lax.broadcasted_iota(jnp.int32, (heads, width), 1)
    block = jnp.where(lax.div(col, head_size) == row, jnp.broadcast_to(wide, (heads, width)), 0.0)
    for i, part in enumerate(split3(block)):
        temp_t[i * heads : (i + 1) * heads, :] = part
    x_t[...] = x_weight[...].astype(f32).T.astype(bf16)
    fx_t[...] = fx_weight[...].astype(f32).T.astype(bf16)

    def own(h):
        return slice(h * head_size, (h + 1) * head_size)

    def step(i, carry):
        here = points[pl.ds(pl.multiple_of(i * FRONT_ROWS, FRONT_ROWS), FRONT_ROWS), :]
        normed = layer_norm(here.astype(f32), gain[...])
        mids[...] = dot_nt(x_t[...], normed).astype(bf16)
        feats[...] = dot_nt(fx_t[...], normed).astype(bf16)
        t = dot(temp_t[...], mids[...])
        t = t[:heads] + t[heads : 2 * heads] + t[2 * heads : 3 * heads]
        temps = 0.5 + jnp.maximum(t, 0.0) + jnp.log(1.0 + jnp.exp(-jnp.abs(t)))
        scales = math.log2(math.e) / temps
        col = lax.broadcasted_iota(jnp.int32, (1, FRONT_ROWS), 1) + i * FRONT_ROWS
        valid = jnp.where(col < live, 1.0, 0.0)
        for q in range(0, heads, 2):
            group = range(q, q + 2)
            logits = [dot(slice_t[...], mids[own(h), :]) for h in group]
            tops = [jnp.max(l, axis=0, keepdims=True) for l in logits]
            raised = [
                jnp.exp2((l - top) * scales[h : h + 1, :]) for h, l, top in zip(group, logits, tops)
            ]
            shares = [valid * pltpu.reciprocal(jnp.sum(r, axis=0, keepdims=True), approx=True) for r in raised]
            for h, r, share in zip(group, raised, shares):
                rows = slice(h * slices, (h + 1) * slices)
                weights = r * share
                stored[i, rows, :] = weights.astype(bf16)
                mass = weights[:, :128]
                for c in range(1, FRONT_ROWS // 128):
                    mass = mass + weights[:, c * 128 : (c + 1) * 128]
                mass_row = jnp.sum(mass.T, axis=0, keepdims=True)
                totals[h // half, span + h % half : span + h % half + 1, :] += mass_row
        for h in range(heads):
            side, at = h // half, h % half
            totals[side, own(at), :] += dot_nt(
                feats[own(h), :], stored[i, h * slices : (h + 1) * slices, :]
            )
        return carry

    lax.fori_loop(0, lax.div(live + FRONT_ROWS - 1, FRONT_ROWS), step, 0)
    keep[...] = totals[core]
    send[...] = totals[1 - core]


def back_kernel(
    sizes, place, stored, mine, theirs, q_weight, k_weight, v_weight, gain, points, out_weight, up, down, *refs
):
    extra = len(refs) - 11
    sent = refs[:extra]
    (
        mixed,
        finished,
        spread,
        desliced,
        crossed,
        value_t,
        repeat,
        tokens,
        queries,
        scores,
        arrived,
    ) = refs[extra:]
    head_size = q_weight.shape[0]
    slices = mine.shape[1]
    half = mine.shape[0] // (head_size + 1)
    span = half * head_size
    heads = 2 * half
    rows, width = points.shape
    piece = up.shape[1] // 2
    live = sizes[place[0]]
    low = place[0] % 2 == 0
    blocks = rows // BACK_ROWS
    def leave(i):
        here = pl.ds(pl.multiple_of(i * BACK_ROWS, BACK_ROWS), BACK_ROWS)
        return pltpu.make_async_copy(finished.at[i], mixed.at[here, :], arrived.at[i])

    def own(h):
        return slice(h * head_size, (h + 1) * head_size)

    tiled = head_tile(dot_nt(k_weight[...], q_weight[...]), half)
    for i, part in enumerate(split3(tiled)):
        crossed[i] = part
    value_t[...] = head_tile(v_weight[...].astype(f32), half).T.astype(bf16)
    row = lax.broadcasted_iota(jnp.int32, (span, half * 128), 0)
    col = lax.broadcasted_iota(jnp.int32, (span, half * 128), 1)
    same = (lax.div(row, head_size) == lax.div(col, 128)) & (
        lax.rem(row, head_size) == lax.rem(col, head_size)
    )
    repeat[...] = jnp.where(same, 1.0, 0.0).astype(bf16)
    queries[...] = jnp.zeros_like(queries)
    for side in range(2):
        sums = jnp.where(low, mine[...], theirs[...]) if side == 0 else jnp.where(low, theirs[...], mine[...])
        parts = []
        for h in range(half):
            mass = sums[span + h : span + h + 1, :] + eps_mass
            parts.append(sums[own(h), :] / mass)
        wide = jnp.concatenate(parts, 0)
        narrow = wide.astype(bf16)
        asked = dot(crossed[0], narrow) + dot(crossed[1], narrow) + dot(crossed[2], narrow)
        for i, part in enumerate(split3(asked * (math.log2(math.e) / math.sqrt(head_size)))):
            for h in range(half):
                queries[side * half + h, own(i), :] = part[own(h), :]
        values = dot(value_t[...], narrow).astype(bf16)
        tokens[...] = dot(narrow.astype(f32).T.astype(bf16), repeat[...]).astype(bf16)
        for h in range(half):
            scores[h] = dot(tokens[:, h * 128 : (h + 1) * 128], queries[side * half + h])
        for h in range(half):
            top = jnp.max(scores[h], axis=0, keepdims=True)
            raised = jnp.exp2(scores[h] - top)
            total = jnp.sum(raised, axis=0, keepdims=True)
            probs = (raised * pltpu.reciprocal(total, approx=True)).astype(bf16)
            spread[own(side * half + h), :] = dot(values[own(h), :], probs).astype(bf16)

    pieces = [
        (up[:, c * piece : (c + 1) * piece], down[c * piece : (c + 1) * piece, :]) for c in range(2)
    ]
    if piece == width:
        pieces += [(r[:width, :], r[width:, :]) for r in sent]
    else:
        pieces += [(sent[2 * i][...], sent[2 * i + 1][...]) for i in range(extra // 2)]

    def step(i, carry):
        per = BACK_ROWS // FRONT_ROWS
        for p in range(per):
            lanes = slice(p * FRONT_ROWS, (p + 1) * FRONT_ROWS)
            for h in range(heads):
                desliced[own(h), lanes] = dot(
                    spread[own(h), :], stored[i * per + p, h * slices : (h + 1) * slices, :]
                )
        picked = desliced[...].T.astype(bf16)
        here = points[pl.ds(pl.multiple_of(i * BACK_ROWS, BACK_ROWS), BACK_ROWS), :]
        residual = here.astype(f32) + dot(picked, out_weight[...])
        late = layer_norm(residual, gain[...])
        total = residual
        raw = dot(late, pieces[0][0])
        for n in range(len(pieces)):
            now = raw
            if n + 1 < len(pieces):
                raw = dot(late, pieces[n + 1][0])
            total = total + dot(gelu(now).astype(bf16), pieces[n][1])
        row = lax.broadcasted_iota(jnp.int32, (BACK_ROWS, 1), 0) + i * BACK_ROWS
        finished[i] = jnp.where(row < live, total, 0.0).astype(bf16)
        leave(i).start()
        return carry

    busy = lax.div(live + BACK_ROWS - 1, BACK_ROWS)
    lax.fori_loop(0, busy, step, 0)
    for i in range(blocks):

        @pl.when(i >= busy)
        def _():
            finished[i] = jnp.zeros_like(finished[i])
            leave(i).start()

    for i in range(blocks):
        leave(i).wait()


SMEM = pl.BlockSpec(memory_space=pltpu.SMEM)
VMEM = pl.BlockSpec(memory_space=pltpu.VMEM)
HBM = pl.BlockSpec(memory_space=pltpu.HBM)


def front_call(sizes, place, points, gain, fx_weight, x_weight, slice_weight, temp_vector):
    rows, width = points.shape
    head_size, slices = slice_weight.shape
    heads = width // head_size
    sums_rows = heads // 2 * (head_size + 1)
    return pl.pallas_call(
        front_kernel,
        in_specs=[SMEM, SMEM] + [VMEM] * 6,
        out_specs=[VMEM, VMEM, VMEM],
        out_shape=[
            jax.ShapeDtypeStruct((rows // FRONT_ROWS, heads * slices, FRONT_ROWS), bf16),
            jax.ShapeDtypeStruct((sums_rows, slices), f32),
            jax.ShapeDtypeStruct((sums_rows, slices), f32),
        ],
        scratch_shapes=[
            pltpu.VMEM((width, width), bf16),
            pltpu.VMEM((width, width), bf16),
            pltpu.VMEM((slices, head_size), bf16),
            pltpu.VMEM((3 * heads, width), bf16),
            pltpu.VMEM((width, FRONT_ROWS), bf16),
            pltpu.VMEM((width, FRONT_ROWS), bf16),
            pltpu.VMEM((2, sums_rows, slices), f32),
        ],
        compiler_params=pltpu.CompilerParams(vmem_limit_bytes=32 * MIB),
        name="front",
    )(
        sizes,
        place,
        gain[None, :],
        slice_weight,
        temp_vector[None, :],
        points,
        fx_weight,
        x_weight,
    )


def back_call(
    sizes, place, stored, mine, theirs, q_weight, k_weight, v_weight, gain, points, out_weight, up, down, sent
):
    rows, width = points.shape
    head_size = q_weight.shape[0]
    slices = mine.shape[1]
    half = mine.shape[0] // (head_size + 1)
    span = half * head_size
    blocks = rows // BACK_ROWS
    return pl.pallas_call(
        back_kernel,
        in_specs=[SMEM, SMEM] + [VMEM] * (11 + len(sent)),
        out_specs=HBM,
        out_shape=jax.ShapeDtypeStruct((rows, width), bf16),
        scratch_shapes=[
            pltpu.VMEM((blocks, BACK_ROWS, width), bf16),
            pltpu.VMEM((2 * span, slices), bf16),
            pltpu.VMEM((width, BACK_ROWS), f32),
            pltpu.VMEM((3, span, span), bf16),
            pltpu.VMEM((span, span), bf16),
            pltpu.VMEM((span, half * 128), bf16),
            pltpu.VMEM((slices, half * 128), bf16),
            pltpu.VMEM((2 * half, 128, slices), bf16),
            pltpu.VMEM((half, slices, slices), f32),
            pltpu.SemaphoreType.DMA((blocks,)),
        ],
        compiler_params=pltpu.CompilerParams(vmem_limit_bytes=36 * MIB),
        name="back",
    )(
        sizes,
        place,
        stored,
        mine,
        theirs,
        q_weight,
        k_weight,
        v_weight,
        gain[None, :],
        points,
        out_weight,
        up,
        down,
        *sent,
    )


def per_device(
    mesh_shape,
    points,
    part_sizes,
    norm1_gain,
    fx_weight,
    x_weight,
    slice_weight,
    temp_vector,
    q_weight,
    k_weight,
    v_weight,
    out_weight,
    norm2_gain,
    up_weight,
    down_weight,
):
    axes = ("pts", "ffn", "sub")
    devices = math.prod(mesh_shape[a] for a in axes)
    shards = mesh_shape["ffn"]
    place = lax.axis_index(axes).astype(jnp.int32).reshape(1)

    piece = up_weight.shape[1] // 2
    core = lax.axis_index("sub")
    halves = (
        lax.dynamic_slice_in_dim(up_weight, core * piece, piece, 1),
        lax.dynamic_slice_in_dim(down_weight, core * piece, piece, 0),
    )
    if piece == up_weight.shape[0]:
        halves = (jnp.concatenate(halves, 0),)
    far_pieces = [
        lax.ppermute(half, "ffn", [(i, (i + turn) % shards) for i in range(shards)])
        for turn in range(1, shards)
        for half in halves
    ]
    stored, keep, send = front_call(
        part_sizes, place, points, norm1_gain, fx_weight, x_weight, slice_weight, temp_vector
    )
    received = lax.ppermute(send, "sub", [(0, 1), (1, 0)])
    bits = [2 << b for b in range((devices // 2).bit_length() - 1)]
    zs = [b for b in bits if b >= 2 * shards]
    xs = [b for b in bits if b < 2 * shards]
    even_order, odd_order = zs[1:] + xs + zs[:1], zs + xs
    sums = keep + received
    for n, (even, odd) in enumerate(zip(even_order, odd_order)):
        if n == 2:
            ready = lax.optimization_barrier((tuple(far_pieces), sums))[0]
            hops = [lax.ppermute(piece, "sub", [(0, 1), (1, 0)]) for piece in ready]
        sums = sums + lax.ppermute(
            sums, axes, [(i, i ^ (odd if i & 1 else even)) for i in range(devices)]
        )
    theirs = lax.ppermute(sums, "sub", [(0, 1), (1, 0)])
    return back_call(
        part_sizes,
        place,
        stored,
        sums,
        theirs,
        q_weight,
        k_weight,
        v_weight,
        norm2_gain,
        points,
        out_weight,
        up_weight,
        down_weight,
        far_pieces + hops,
    )


def solution(mesh):
    return jax.shard_map(
        functools.partial(per_device, dict(mesh.shape)),
        mesh=mesh,
        in_specs=(
            P(("groups", "pts", "ffn", "sub"), None),
            P("groups"),
            P(),
            P(),
            P(),
            P(),
            P(),
            P(),
            P(),
            P(),
            P(),
            P(),
            P(None, "ffn"),
            P("ffn", None),
        ),
        out_specs=P(("groups", "pts", "ffn", "sub"), None),
        check_vma=False,
    )
```

```python
import functools
import math

import jax
import jax.numpy as jnp
from jax import lax
from jax.experimental import pallas as pl
from jax.experimental.pallas import tpu as pltpu
from jax.sharding import PartitionSpec as P

eps_norm = 1e-05
eps_mass = 1e-05
f32 = jnp.float32
bf16 = jnp.bfloat16
MIB = 1024 * 1024
FRONT_ROWS = 512
BACK_ROWS = 512


def dot(a, b):
    return jnp.dot(a, b, preferred_element_type=f32)


def dot_nt(a, b):
    return lax.dot_general(a, b, (((1,), (1,)), ((), ())), preferred_element_type=f32)


def split3(x):
    first = x.astype(bf16)
    rest = x - first.astype(f32)
    second = rest.astype(bf16)
    third = (rest - second.astype(f32)).astype(bf16)
    return first, second, third


def layer_norm(wide, gain):
    centered = wide - jnp.mean(wide, axis=-1, keepdims=True)
    variance = jnp.mean(centered * centered, axis=-1, keepdims=True)
    return (centered * lax.rsqrt(variance + eps_norm) * gain).astype(bf16)


def gelu(x):
    halved = 0.5 * x
    return halved + halved * lax.erf(x * math.sqrt(0.5))


def head_tile(weight, copies):
    size = weight.shape[0]
    wide = jnp.concatenate([weight] * copies, 1)
    tall = jnp.concatenate([wide] * copies, 0)
    row = lax.broadcasted_iota(jnp.int32, tall.shape, 0)
    col = lax.broadcasted_iota(jnp.int32, tall.shape, 1)
    return jnp.where(lax.div(row, size) == lax.div(col, size), tall, 0.0)


def front_kernel(
    sizes,
    place,
    gain,
    slice_weight,
    temp_vector,
    points,
    fx_weight,
    x_weight,
    stored,
    keep,
    send,
    fx_t,
    x_t,
    slice_t,
    temp_t,
    feats,
    mids,
    totals,
):
    head_size, slices = slice_weight.shape
    width = points.shape[1]
    heads = width // head_size
    half = heads // 2
    span = half * head_size
    live = sizes[place[0]]
    core = place[0] % 2
    totals[...] = jnp.zeros_like(totals)
    slice_t[...] = slice_weight[...].astype(f32).T.astype(bf16)
    wide = jnp.concatenate([temp_vector[...]] * heads, 1)
    row = lax.broadcasted_iota(jnp.int32, (heads, width), 0)
    col = lax.broadcasted_iota(jnp.int32, (heads, width), 1)
    block = jnp.where(lax.div(col, head_size) == row, jnp.broadcast_to(wide, (heads, width)), 0.0)
    for i, part in enumerate(split3(block)):
        temp_t[i * heads : (i + 1) * heads, :] = part
    x_t[...] = x_weight[...].astype(f32).T.astype(bf16)
    fx_t[...] = fx_weight[...].astype(f32).T.astype(bf16)

    def own(h):
        return slice(h * head_size, (h + 1) * head_size)

    def add_sums(i, h):
        totals[h // half, own(h % half), :] += dot_nt(
            feats[own(h), :], stored[i, h * slices : (h + 1) * slices, :]
        )

    def step(i, carry):
        here = points[pl.ds(pl.multiple_of(i * FRONT_ROWS, FRONT_ROWS), FRONT_ROWS), :]
        normed = layer_norm(here.astype(f32), gain[...])
        mids[...] = dot_nt(x_t[...], normed).astype(bf16)
        feats[...] = dot_nt(fx_t[...], normed).astype(bf16)
        t = dot(temp_t[...], mids[...])
        t = t[:heads] + t[heads : 2 * heads] + t[2 * heads : 3 * heads]
        temps = 0.5 + jnp.maximum(t, 0.0) + jnp.log(1.0 + jnp.exp(-jnp.abs(t)))
        scales = math.log2(math.e) / temps
        col = lax.broadcasted_iota(jnp.int32, (1, FRONT_ROWS), 1) + i * FRONT_ROWS
        valid = jnp.where(col < live, 1.0, 0.0)
        for q in range(0, heads, 2):
            group = range(q, q + 2)
            logits = [dot(slice_t[...], mids[own(h), :]) for h in group]
            if q:
                add_sums(i, q - 2)
                add_sums(i, q - 1)
            tops = [jnp.max(l, axis=0, keepdims=True) for l in logits]
            raised = [
                jnp.exp2((l - top) * scales[h : h + 1, :]) for h, l, top in zip(group, logits, tops)
            ]
            shares = [valid * pltpu.reciprocal(jnp.sum(r, axis=0, keepdims=True), approx=True) for r in raised]
            for h, r, share in zip(group, raised, shares):
                weights = r * share
                stored[i, h * slices : (h + 1) * slices, :] = weights.astype(bf16)
                mass = weights[:, :128]
                for c in range(1, FRONT_ROWS // 128):
                    mass = mass + weights[:, c * 128 : (c + 1) * 128]
                mass_row = jnp.sum(mass.T, axis=0, keepdims=True)
                totals[h // half, span + h % half : span + h % half + 1, :] += mass_row
        add_sums(i, heads - 2)
        add_sums(i, heads - 1)
        return carry

    lax.fori_loop(0, lax.div(live + FRONT_ROWS - 1, FRONT_ROWS), step, 0)
    keep[...] = totals[core]
    send[...] = totals[1 - core]


def mix_tokens(sums, crossed, value_t, repeat, tokens, queries, scores, probs, spread, at):
    slices = sums.shape[1]
    span = value_t.shape[0]
    half = scores.shape[0]
    head_size = span // half

    def own(h):
        return slice(h * head_size, (h + 1) * head_size)

    parts = []
    for h in range(half):
        mass = sums[span + h : span + h + 1, :] + eps_mass
        parts.append(sums[own(h), :] / mass)
    wide = jnp.concatenate(parts, 0)
    narrow = wide.astype(bf16)
    asked = dot(crossed[0], narrow) + dot(crossed[1], narrow) + dot(crossed[2], narrow)
    for i, part in enumerate(split3(asked * (math.log2(math.e) / math.sqrt(head_size)))):
        for h in range(half):
            queries[h, own(i), :] = part[own(h), :]
    values = dot(value_t[...], narrow).astype(bf16)
    tokens[...] = dot(narrow.astype(f32).T.astype(bf16), repeat[...]).astype(bf16)
    for h in range(half):
        scores[h] = dot(tokens[:, h * 128 : (h + 1) * 128], queries[h])
    for h in range(half):
        top = jnp.max(scores[h], axis=0, keepdims=True)
        raised = jnp.exp2(scores[h] - top)
        total = jnp.sum(raised, axis=0, keepdims=True)
        probs[h] = (raised * pltpu.reciprocal(total, approx=True)).astype(bf16)
        if h:
            spread[at + (h - 1) * head_size : at + h * head_size, :] = dot(
                values[own(h - 1), :], probs[h - 1]
            ).astype(bf16)
    spread[at + span - head_size : at + span, :] = dot(values[own(half - 1), :], probs[half - 1]).astype(bf16)


def mix_weights(q_weight, k_weight, v_weight, crossed, value_t, repeat, queries):
    half, head_size = queries.shape[0], q_weight.shape[0]
    span = half * head_size
    tiled = head_tile(dot_nt(k_weight[...], q_weight[...]), half)
    for i, part in enumerate(split3(tiled)):
        crossed[i] = part
    value_t[...] = head_tile(v_weight[...].astype(f32), half).T.astype(bf16)
    row = lax.broadcasted_iota(jnp.int32, (span, half * 128), 0)
    col = lax.broadcasted_iota(jnp.int32, (span, half * 128), 1)
    same = (lax.div(row, head_size) == lax.div(col, 128)) & (
        lax.rem(row, head_size) == lax.rem(col, head_size)
    )
    repeat[...] = jnp.where(same, 1.0, 0.0).astype(bf16)
    queries[...] = jnp.zeros_like(queries)


def mix_kernel(sums, q_weight, k_weight, v_weight, out, crossed, value_t, repeat, tokens, queries, scores, probs):
    mix_weights(q_weight, k_weight, v_weight, crossed, value_t, repeat, queries)
    mix_tokens(sums, crossed, value_t, repeat, tokens, queries, scores, probs, out, 0)


def mix_scratch(half, head_size, slices):
    span = half * head_size
    return [
        pltpu.VMEM((3, span, span), bf16),
        pltpu.VMEM((span, span), bf16),
        pltpu.VMEM((span, half * 128), bf16),
        pltpu.VMEM((slices, half * 128), bf16),
        pltpu.VMEM((half, 128, slices), bf16),
        pltpu.VMEM((half, slices, slices), f32),
        pltpu.VMEM((half, slices, slices), bf16),
    ]


def back_kernel(
    sizes, place, stored, mine, theirs, q_weight, k_weight, v_weight, gain, points, out_weight, up, down, *refs
):
    extra = len(refs) - 13
    sent = refs[:extra]
    (
        mixed,
        finished,
        spread,
        mixed_here,
        desliced,
        crossed,
        value_t,
        repeat,
        tokens,
        queries,
        scores,
        probs,
        arrived,
    ) = refs[extra:]
    head_size = q_weight.shape[0]
    slices = mine.shape[1]
    span = mine.shape[0]
    half = span // head_size
    heads = 2 * half
    rows, width = points.shape
    piece = up.shape[1] // 2
    live = sizes[place[0]]
    low = place[0] % 2 == 0
    blocks = rows // BACK_ROWS
    def leave(i):
        here = pl.ds(pl.multiple_of(i * BACK_ROWS, BACK_ROWS), BACK_ROWS)
        return pltpu.make_async_copy(finished.at[i], mixed.at[here, :], arrived.at[i])

    def own(h):
        return slice(h * head_size, (h + 1) * head_size)

    mix_weights(q_weight, k_weight, v_weight, crossed, value_t, repeat, queries)
    mix_tokens(theirs, crossed, value_t, repeat, tokens, queries, scores, probs, mixed_here, 0)
    own_side, other_side = mine[...].astype(f32), mixed_here[...].astype(f32)
    spread[:span, :] = jnp.where(low, own_side, other_side).astype(bf16)
    spread[span:, :] = jnp.where(low, other_side, own_side).astype(bf16)

    pieces = [
        (up.at[:, pl.ds(c * piece, piece)], down.at[pl.ds(c * piece, piece), :]) for c in range(2)
    ]
    if piece == width:
        pieces += [(r.at[pl.ds(0, width), :], r.at[pl.ds(width, piece), :]) for r in sent]
    else:
        pieces += [(sent[2 * i], sent[2 * i + 1]) for i in range(extra // 2)]

    def step(i, carry):
        per = BACK_ROWS // FRONT_ROWS
        for p in range(per):
            lanes = slice(p * FRONT_ROWS, (p + 1) * FRONT_ROWS)
            for h in range(heads):
                desliced[own(h), lanes] = dot(
                    spread[own(h), :], stored[i * per + p, h * slices : (h + 1) * slices, :]
                )
        picked = desliced[...].T.astype(bf16)
        here = points[pl.ds(pl.multiple_of(i * BACK_ROWS, BACK_ROWS), BACK_ROWS), :]
        residual = here.astype(f32) + dot(picked, out_weight[...])
        late = layer_norm(residual, gain[...])
        total = residual
        raw = dot(late, pieces[0][0][...])
        for n in range(len(pieces)):
            now = raw
            if n + 1 < len(pieces):
                raw = dot(late, pieces[n + 1][0][...])
            total = total + dot(gelu(now).astype(bf16), pieces[n][1][...])
        row = lax.broadcasted_iota(jnp.int32, (BACK_ROWS, 1), 0) + i * BACK_ROWS
        finished[i] = jnp.where(row < live, total, 0.0).astype(bf16)
        leave(i).start()
        return carry

    busy = lax.div(live + BACK_ROWS - 1, BACK_ROWS)
    lax.fori_loop(0, busy, step, 0)
    for i in range(blocks):

        @pl.when(i >= busy)
        def _():
            finished[i] = jnp.zeros_like(finished[i])
            leave(i).start()

    for i in range(blocks):
        leave(i).wait()


SMEM = pl.BlockSpec(memory_space=pltpu.SMEM)
VMEM = pl.BlockSpec(memory_space=pltpu.VMEM)
HBM = pl.BlockSpec(memory_space=pltpu.HBM)


def front_call(sizes, place, points, gain, fx_weight, x_weight, slice_weight, temp_vector):
    rows, width = points.shape
    head_size, slices = slice_weight.shape
    heads = width // head_size
    sums_rows = heads // 2 * (head_size + 1)
    return pl.pallas_call(
        front_kernel,
        in_specs=[SMEM, SMEM] + [VMEM] * 6,
        out_specs=[VMEM, VMEM, VMEM],
        out_shape=[
            jax.ShapeDtypeStruct((rows // FRONT_ROWS, heads * slices, FRONT_ROWS), bf16),
            jax.ShapeDtypeStruct((sums_rows, slices), f32),
            jax.ShapeDtypeStruct((sums_rows, slices), f32),
        ],
        scratch_shapes=[
            pltpu.VMEM((width, width), bf16),
            pltpu.VMEM((width, width), bf16),
            pltpu.VMEM((slices, head_size), bf16),
            pltpu.VMEM((3 * heads, width), bf16),
            pltpu.VMEM((width, FRONT_ROWS), bf16),
            pltpu.VMEM((width, FRONT_ROWS), bf16),
            pltpu.VMEM((2, sums_rows, slices), f32),
        ],
        compiler_params=pltpu.CompilerParams(vmem_limit_bytes=32 * MIB),
        name="front",
    )(
        sizes,
        place,
        gain[None, :],
        slice_weight,
        temp_vector[None, :],
        points,
        fx_weight,
        x_weight,
    )


def mix_call(sums, q_weight, k_weight, v_weight):
    head_size = q_weight.shape[0]
    slices = sums.shape[1]
    half = sums.shape[0] // (head_size + 1)
    return pl.pallas_call(
        mix_kernel,
        in_specs=[VMEM] * 4,
        out_specs=VMEM,
        out_shape=jax.ShapeDtypeStruct((half * head_size, slices), bf16),
        scratch_shapes=mix_scratch(half, head_size, slices),
        compiler_params=pltpu.CompilerParams(vmem_limit_bytes=12 * MIB),
        cost_estimate=pl.CostEstimate(flops=300_000_000, bytes_accessed=500_000, transcendentals=600_000),
        name="mix",
    )(sums, q_weight, k_weight, v_weight)


def back_call(
    sizes, place, stored, mine, theirs, q_weight, k_weight, v_weight, gain, points, out_weight, up, down, sent
):
    rows, width = points.shape
    head_size = q_weight.shape[0]
    slices = mine.shape[1]
    span = mine.shape[0]
    half = span // head_size
    blocks = rows // BACK_ROWS
    return pl.pallas_call(
        back_kernel,
        in_specs=[SMEM, SMEM] + [VMEM] * (11 + len(sent)),
        out_specs=HBM,
        out_shape=jax.ShapeDtypeStruct((rows, width), bf16),
        scratch_shapes=[
            pltpu.VMEM((blocks, BACK_ROWS, width), bf16),
            pltpu.VMEM((2 * span, slices), bf16),
            pltpu.VMEM((span, slices), bf16),
            pltpu.VMEM((width, BACK_ROWS), f32),
            *mix_scratch(half, head_size, slices),
            pltpu.SemaphoreType.DMA((blocks,)),
        ],
        compiler_params=pltpu.CompilerParams(vmem_limit_bytes=36 * MIB),
        name="back",
    )(
        sizes,
        place,
        stored,
        mine,
        theirs,
        q_weight,
        k_weight,
        v_weight,
        gain[None, :],
        points,
        out_weight,
        up,
        down,
        *sent,
    )


def per_device(
    mesh_shape,
    points,
    part_sizes,
    norm1_gain,
    fx_weight,
    x_weight,
    slice_weight,
    temp_vector,
    q_weight,
    k_weight,
    v_weight,
    out_weight,
    norm2_gain,
    up_weight,
    down_weight,
):
    axes = ("pts", "ffn", "sub")
    devices = math.prod(mesh_shape[a] for a in axes)
    shards = mesh_shape["ffn"]
    place = lax.axis_index(axes).astype(jnp.int32).reshape(1)

    piece = up_weight.shape[1] // 2
    core = lax.axis_index("sub")
    halves = (
        lax.dynamic_slice_in_dim(up_weight, core * piece, piece, 1),
        lax.dynamic_slice_in_dim(down_weight, core * piece, piece, 0),
    )
    if piece == up_weight.shape[0]:
        halves = (jnp.concatenate(halves, 0),)
    far_pieces = [
        lax.ppermute(half, "ffn", [(i, (i + turn) % shards) for i in range(shards)])
        for turn in range(1, shards)
        for half in halves
    ]
    stored, keep, send = front_call(
        part_sizes, place, points, norm1_gain, fx_weight, x_weight, slice_weight, temp_vector
    )
    received = lax.ppermute(send, "sub", [(0, 1), (1, 0)])
    bits = [2 << b for b in range((devices // 2).bit_length() - 1)]
    zs = [b for b in bits if b >= 2 * shards]
    xs = [b for b in bits if b < 2 * shards]
    even_order, odd_order = zs[1:] + xs + zs[:1], zs + xs
    sums = keep + received
    for n, (even, odd) in enumerate(zip(even_order, odd_order)):
        if n == 2:
            ready = lax.optimization_barrier((tuple(far_pieces), sums))[0]
            hops = [lax.ppermute(piece, "sub", [(0, 1), (1, 0)]) for piece in ready]
        sums = sums + lax.ppermute(
            sums, axes, [(i, i ^ (odd if i & 1 else even)) for i in range(devices)]
        )
    theirs = lax.ppermute(sums, "sub", [(0, 1), (1, 0)])
    mine = mix_call(sums, q_weight, k_weight, v_weight)
    return back_call(
        part_sizes,
        place,
        stored,
        mine,
        theirs,
        q_weight,
        k_weight,
        v_weight,
        norm2_gain,
        points,
        out_weight,
        up_weight,
        down_weight,
        far_pieces + hops,
    )


def solution(mesh):
    return jax.shard_map(
        functools.partial(per_device, dict(mesh.shape)),
        mesh=mesh,
        in_specs=(
            P(("groups", "pts", "ffn", "sub"), None),
            P("groups"),
            P(),
            P(),
            P(),
            P(),
            P(),
            P(),
            P(),
            P(),
            P(),
            P(),
            P(None, "ffn"),
            P("ffn", None),
        ),
        out_specs=P(("groups", "pts", "ffn", "sub"), None),
        check_vma=False,
    )
```

```python
import functools
import math

import jax
import jax.numpy as jnp
from jax import lax
from jax.experimental import pallas as pl
from jax.experimental.pallas import tpu as pltpu
from jax.sharding import PartitionSpec as P

eps_norm = 1e-05
eps_mass = 1e-05
f32 = jnp.float32
bf16 = jnp.bfloat16
MIB = 1024 * 1024
FRONT_ROWS = 512
BACK_ROWS = 512


def dot(a, b):
    return jnp.dot(a, b, preferred_element_type=f32)


def dot_nt(a, b):
    return lax.dot_general(a, b, (((1,), (1,)), ((), ())), preferred_element_type=f32)


def split3(x):
    first = x.astype(bf16)
    rest = x - first.astype(f32)
    second = rest.astype(bf16)
    third = (rest - second.astype(f32)).astype(bf16)
    return first, second, third


def layer_norm(wide, gain):
    centered = wide - jnp.mean(wide, axis=-1, keepdims=True)
    variance = jnp.mean(centered * centered, axis=-1, keepdims=True)
    return (centered * lax.rsqrt(variance + eps_norm) * gain).astype(bf16)


def gelu(x):
    halved = 0.5 * x
    return halved + halved * lax.erf(x * math.sqrt(0.5))


def head_tile(weight, copies):
    size = weight.shape[0]
    wide = jnp.concatenate([weight] * copies, 1)
    tall = jnp.concatenate([wide] * copies, 0)
    row = lax.broadcasted_iota(jnp.int32, tall.shape, 0)
    col = lax.broadcasted_iota(jnp.int32, tall.shape, 1)
    return jnp.where(lax.div(row, size) == lax.div(col, size), tall, 0.0)


def front_kernel(
    zunit,
    sizes,
    place,
    gain,
    slice_weight,
    temp_vector,
    points,
    fx_weight,
    x_weight,
    stored,
    keep,
    send,
    fx_t,
    x_t,
    slice_t,
    temp_t,
    feats,
    mids,
    totals,
):
    head_size, slices = slice_weight.shape
    width = points.shape[1]
    heads = width // head_size
    quarter = heads // 4
    live = sizes[place[0]]
    core, turn = place[0] % 2, lax.div(place[0], zunit) % 2
    totals[...] = jnp.zeros_like(totals)
    slice_t[...] = slice_weight[...].astype(f32).T.astype(bf16)
    wide = jnp.concatenate([temp_vector[...]] * heads, 1)
    row = lax.broadcasted_iota(jnp.int32, (heads, width), 0)
    col = lax.broadcasted_iota(jnp.int32, (heads, width), 1)
    block = jnp.where(lax.div(col, head_size) == row, jnp.broadcast_to(wide, (heads, width)), 0.0)
    for i, part in enumerate(split3(block)):
        temp_t[i * heads : (i + 1) * heads, :] = part
    x_t[...] = x_weight[...].astype(f32).T.astype(bf16)
    fx_t[...] = fx_weight[...].astype(f32).T.astype(bf16)

    def own(h):
        return slice(h * head_size, (h + 1) * head_size)

    def add_sums(i, h):
        totals[h // quarter, own(h % quarter), :] += dot_nt(
            feats[own(h), :], stored[i, h * slices : (h + 1) * slices, :]
        )

    def step(i, carry):
        here = points[pl.ds(pl.multiple_of(i * FRONT_ROWS, FRONT_ROWS), FRONT_ROWS), :]
        normed = layer_norm(here.astype(f32), gain[...])
        mids[...] = dot_nt(x_t[...], normed).astype(bf16)
        feats[...] = dot_nt(fx_t[...], normed).astype(bf16)
        t = dot(temp_t[...], mids[...])
        t = t[:heads] + t[heads : 2 * heads] + t[2 * heads : 3 * heads]
        temps = 0.5 + jnp.maximum(t, 0.0) + jnp.log(1.0 + jnp.exp(-jnp.abs(t)))
        scales = math.log2(math.e) / temps
        col = lax.broadcasted_iota(jnp.int32, (1, FRONT_ROWS), 1) + i * FRONT_ROWS
        valid = jnp.where(col < live, 1.0, 0.0)
        for q in range(0, heads, 1):
            group = range(q, q + 1)
            logits = [dot(slice_t[...], mids[own(h), :]) for h in group]
            if q:
                for h in range(q - 1, q):
                    add_sums(i, h)
            tops = [jnp.max(l, axis=0, keepdims=True) for l in logits]
            raised = [
                jnp.exp2((l - top) * scales[h : h + 1, :]) for h, l, top in zip(group, logits, tops)
            ]
            shares = [valid * pltpu.reciprocal(jnp.sum(r, axis=0, keepdims=True), approx=True) for r in raised]
            for h, r, share in zip(group, raised, shares):
                weights = r * share
                stored[i, h * slices : (h + 1) * slices, :] = weights.astype(bf16)
                mass = weights[:, :128]
                for c in range(1, FRONT_ROWS // 128):
                    mass = mass + weights[:, c * 128 : (c + 1) * 128]
                mass_row = jnp.sum(mass.T, axis=0, keepdims=True)
                at = quarter * head_size + h % quarter
                totals[h // quarter, at : at + 1, :] += mass_row
        for h in range(heads - 1, heads):
            add_sums(i, h)
        return carry

    lax.fori_loop(0, lax.div(live + FRONT_ROWS - 1, FRONT_ROWS), step, 0)
    for n in range(2):
        keep[n] = totals[2 * core + (turn if n == 0 else 1 - turn)]
        send[n] = totals[2 * (1 - core) + (turn if n == 0 else 1 - turn)]


def mix_tokens(sums, crossed, value_t, repeat, tokens, queries, scores, probs, spread, at):
    slices = sums.shape[1]
    span = value_t.shape[0]
    half = scores.shape[0]
    head_size = span // half

    def own(h):
        return slice(h * head_size, (h + 1) * head_size)

    parts = []
    for h in range(half):
        mass = sums[span + h : span + h + 1, :] + eps_mass
        parts.append(sums[own(h), :] / mass)
    wide = jnp.concatenate(parts, 0)
    narrow = wide.astype(bf16)
    asked = dot(crossed[0], narrow) + dot(crossed[1], narrow) + dot(crossed[2], narrow)
    for i, part in enumerate(split3(asked * (math.log2(math.e) / math.sqrt(head_size)))):
        for h in range(half):
            queries[h, own(i), :] = part[own(h), :]
    values = dot(value_t[...], narrow).astype(bf16)
    tokens[...] = dot(narrow.astype(f32).T.astype(bf16), repeat[...]).astype(bf16)
    for h in range(half):
        scores[h] = dot(tokens[:, h * 128 : (h + 1) * 128], queries[h])
    for h in range(half):
        top = jnp.max(scores[h], axis=0, keepdims=True)
        raised = jnp.exp2(scores[h] - top)
        total = jnp.sum(raised, axis=0, keepdims=True)
        probs[h] = (raised * pltpu.reciprocal(total, approx=True)).astype(bf16)
        if h:
            spread[at + (h - 1) * head_size : at + h * head_size, :] = dot(
                values[own(h - 1), :], probs[h - 1]
            ).astype(bf16)
    spread[at + span - head_size : at + span, :] = dot(values[own(half - 1), :], probs[half - 1]).astype(bf16)


def mix_weights(q_weight, k_weight, v_weight, crossed, value_t, repeat, queries):
    half, head_size = queries.shape[0], q_weight.shape[0]
    span = half * head_size
    tiled = head_tile(dot_nt(k_weight[...], q_weight[...]), half)
    for i, part in enumerate(split3(tiled)):
        crossed[i] = part
    value_t[...] = head_tile(v_weight[...].astype(f32), half).T.astype(bf16)
    row = lax.broadcasted_iota(jnp.int32, (span, half * 128), 0)
    col = lax.broadcasted_iota(jnp.int32, (span, half * 128), 1)
    same = (lax.div(row, head_size) == lax.div(col, 128)) & (
        lax.rem(row, head_size) == lax.rem(col, head_size)
    )
    repeat[...] = jnp.where(same, 1.0, 0.0).astype(bf16)
    queries[...] = jnp.zeros_like(queries)


def mix_kernel(sums, q_weight, k_weight, v_weight, out, crossed, value_t, repeat, tokens, queries, scores, probs):
    mix_weights(q_weight, k_weight, v_weight, crossed, value_t, repeat, queries)
    mix_tokens(sums, crossed, value_t, repeat, tokens, queries, scores, probs, out, 0)


def mix_scratch(half, head_size, slices):
    span = half * head_size
    return [
        pltpu.VMEM((3, span, span), bf16),
        pltpu.VMEM((span, span), bf16),
        pltpu.VMEM((span, half * 128), bf16),
        pltpu.VMEM((slices, half * 128), bf16),
        pltpu.VMEM((half, 128, slices), bf16),
        pltpu.VMEM((half, slices, slices), f32),
        pltpu.VMEM((half, slices, slices), bf16),
    ]


def back_kernel(
    zunit, sizes, place, stored, mine, across, along, corner, gain, points, out_weight, up, down, *refs
):
    extra = len(refs) - 5
    sent = refs[:extra]
    mixed, finished, spread, desliced, arrived = refs[extra:]
    span, slices = mine.shape
    rows, width = points.shape
    heads = stored.shape[1] // slices
    head_size = width // heads
    piece = up.shape[1] // 2
    live = sizes[place[0]]
    low = place[0] % 2 == 0
    near = lax.div(place[0], zunit) % 2 == 0
    blocks = rows // BACK_ROWS
    def leave(i):
        here = pl.ds(pl.multiple_of(i * BACK_ROWS, BACK_ROWS), BACK_ROWS)
        return pltpu.make_async_copy(finished.at[i], mixed.at[here, :], arrived.at[i])

    def own(h):
        return slice(h * head_size, (h + 1) * head_size)

    wide = [piece[...].astype(f32) for piece in (mine, across, along, corner)]
    for side in range(2):
        here = [jnp.where(low, wide[n + side], wide[n + 1 - side]) for n in (0, 2)]
        for part in range(2):
            at = (2 * side + part) * span
            spread[at : at + span, :] = jnp.where(near, here[part], here[1 - part]).astype(bf16)

    pieces = [
        (up.at[:, pl.ds(c * piece, piece)], down.at[pl.ds(c * piece, piece), :]) for c in range(2)
    ]
    if piece == width:
        pieces += [(r.at[pl.ds(0, width), :], r.at[pl.ds(width, piece), :]) for r in sent]
    else:
        pieces += [(sent[2 * i], sent[2 * i + 1]) for i in range(extra // 2)]

    def step(i, carry):
        per = BACK_ROWS // FRONT_ROWS
        for p in range(per):
            lanes = slice(p * FRONT_ROWS, (p + 1) * FRONT_ROWS)
            for h in range(heads):
                desliced[own(h), lanes] = dot(
                    spread[own(h), :], stored[i * per + p, h * slices : (h + 1) * slices, :]
                )
        picked = desliced[...].T.astype(bf16)
        here = points[pl.ds(pl.multiple_of(i * BACK_ROWS, BACK_ROWS), BACK_ROWS), :]
        residual = here.astype(f32) + dot(picked, out_weight[...])
        late = layer_norm(residual, gain[...])
        total = residual
        raw = dot(late, pieces[0][0][...])
        for n in range(len(pieces)):
            now = raw
            if n + 1 < len(pieces):
                raw = dot(late, pieces[n + 1][0][...])
            total = total + dot(gelu(now).astype(bf16), pieces[n][1][...])
        row = lax.broadcasted_iota(jnp.int32, (BACK_ROWS, 1), 0) + i * BACK_ROWS
        finished[i] = jnp.where(row < live, total, 0.0).astype(bf16)
        leave(i).start()
        return carry

    busy = lax.div(live + BACK_ROWS - 1, BACK_ROWS)
    lax.fori_loop(0, busy, step, 0)
    for i in range(blocks):

        @pl.when(i >= busy)
        def _():
            finished[i] = jnp.zeros_like(finished[i])
            leave(i).start()

    for i in range(blocks):
        leave(i).wait()


SMEM = pl.BlockSpec(memory_space=pltpu.SMEM)
VMEM = pl.BlockSpec(memory_space=pltpu.VMEM)
HBM = pl.BlockSpec(memory_space=pltpu.HBM)


def front_call(zunit, sizes, place, points, gain, fx_weight, x_weight, slice_weight, temp_vector):
    rows, width = points.shape
    head_size, slices = slice_weight.shape
    heads = width // head_size
    sums_rows = -(-(heads // 4 * (head_size + 1)) // 8) * 8
    return pl.pallas_call(
        functools.partial(front_kernel, zunit),
        in_specs=[SMEM, SMEM] + [VMEM] * 6,
        out_specs=[VMEM, VMEM, VMEM],
        out_shape=[
            jax.ShapeDtypeStruct((rows // FRONT_ROWS, heads * slices, FRONT_ROWS), bf16),
            jax.ShapeDtypeStruct((2, sums_rows, slices), f32),
            jax.ShapeDtypeStruct((2, sums_rows, slices), f32),
        ],
        scratch_shapes=[
            pltpu.VMEM((width, width), bf16),
            pltpu.VMEM((width, width), bf16),
            pltpu.VMEM((slices, head_size), bf16),
            pltpu.VMEM((3 * heads, width), bf16),
            pltpu.VMEM((width, FRONT_ROWS), bf16),
            pltpu.VMEM((width, FRONT_ROWS), bf16),
            pltpu.VMEM((4, sums_rows, slices), f32),
        ],
        compiler_params=pltpu.CompilerParams(vmem_limit_bytes=32 * MIB),
        name="front",
    )(
        sizes,
        place,
        gain[None, :],
        slice_weight,
        temp_vector[None, :],
        points,
        fx_weight,
        x_weight,
    )


def mix_call(sums, q_weight, k_weight, v_weight):
    head_size = q_weight.shape[0]
    slices = sums.shape[1]
    half = sums.shape[0] // (head_size + 1)
    return pl.pallas_call(
        mix_kernel,
        in_specs=[VMEM] * 4,
        out_specs=VMEM,
        out_shape=jax.ShapeDtypeStruct((half * head_size, slices), bf16),
        scratch_shapes=mix_scratch(half, head_size, slices),
        compiler_params=pltpu.CompilerParams(vmem_limit_bytes=12 * MIB),
        cost_estimate=pl.CostEstimate(flops=300_000_000, bytes_accessed=500_000, transcendentals=600_000),
        name="mix",
    )(sums, q_weight, k_weight, v_weight)


def back_call(zunit, sizes, place, stored, tokens, gain, points, out_weight, up, down, sent):
    rows, width = points.shape
    slices = tokens[0].shape[1]
    blocks = rows // BACK_ROWS
    return pl.pallas_call(
        functools.partial(back_kernel, zunit),
        in_specs=[SMEM, SMEM] + [VMEM] * (10 + len(sent)),
        out_specs=HBM,
        out_shape=jax.ShapeDtypeStruct((rows, width), bf16),
        scratch_shapes=[
            pltpu.VMEM((blocks, BACK_ROWS, width), bf16),
            pltpu.VMEM((width, slices), bf16),
            pltpu.VMEM((width, BACK_ROWS), f32),
            pltpu.SemaphoreType.DMA((blocks,)),
        ],
        compiler_params=pltpu.CompilerParams(vmem_limit_bytes=36 * MIB),
        name="back",
    )(
        sizes,
        place,
        stored,
        *tokens,
        gain[None, :],
        points,
        out_weight,
        up,
        down,
        *sent,
    )


def per_device(
    mesh_shape,
    points,
    part_sizes,
    norm1_gain,
    fx_weight,
    x_weight,
    slice_weight,
    temp_vector,
    q_weight,
    k_weight,
    v_weight,
    out_weight,
    norm2_gain,
    up_weight,
    down_weight,
):
    axes = ("pts", "ffn", "sub")
    devices = math.prod(mesh_shape[a] for a in axes)
    shards = mesh_shape["ffn"]
    place = lax.axis_index(axes).astype(jnp.int32).reshape(1)

    piece = up_weight.shape[1] // 2
    core = lax.axis_index("sub")
    halves = (
        lax.dynamic_slice_in_dim(up_weight, core * piece, piece, 1),
        lax.dynamic_slice_in_dim(down_weight, core * piece, piece, 0),
    )
    if piece == up_weight.shape[0]:
        halves = (jnp.concatenate(halves, 0),)
    far_pieces = [
        lax.ppermute(half, "ffn", [(i, (i + turn) % shards) for i in range(shards)])
        for turn in range(1, shards)
        for half in halves
    ]
    zunit = 2 * shards
    stored, keep, send = front_call(
        zunit, part_sizes, place, points, norm1_gain, fx_weight, x_weight, slice_weight, temp_vector
    )
    received = lax.ppermute(send, "sub", [(0, 1), (1, 0)])
    bits = [2 << b for b in range((devices // 2).bit_length() - 1)]
    zs = [b for b in bits if b > zunit]
    xs = [b for b in bits if b < zunit]

    def swap(x, even, odd):
        return lax.ppermute(x, axes, [(i, i ^ (odd if i & 1 else even)) for i in range(devices)])

    sums = keep[0] + received[0] + swap(keep[1] + received[1], zunit, zunit)
    for n, (even, odd) in enumerate(zip(zs + xs, xs + zs)):
        if n == len(zs + xs) - 1:
            ready = lax.optimization_barrier((tuple(far_pieces), sums))[0]
            hops = [lax.ppermute(piece, "sub", [(0, 1), (1, 0)]) for piece in ready]
        sums = sums + swap(sums, even, odd)
    mine = mix_call(sums, q_weight, k_weight, v_weight)
    along = swap(mine, zunit, zunit)
    pair = lax.ppermute(jnp.stack([mine, along]), "sub", [(0, 1), (1, 0)])
    tokens = [mine, pair[0], along, pair[1]]
    return back_call(
        zunit,
        part_sizes,
        place,
        stored,
        tokens,
        norm2_gain,
        points,
        out_weight,
        up_weight,
        down_weight,
        far_pieces + hops,
    )


def solution(mesh):
    return jax.shard_map(
        functools.partial(per_device, dict(mesh.shape)),
        mesh=mesh,
        in_specs=(
            P(("groups", "pts", "ffn", "sub"), None),
            P("groups"),
            P(),
            P(),
            P(),
            P(),
            P(),
            P(),
            P(),
            P(),
            P(),
            P(),
            P(None, "ffn"),
            P("ffn", None),
        ),
        out_specs=P(("groups", "pts", "ffn", "sub"), None),
        check_vma=False,
    )
```

```python
import functools
import math

import jax
import jax.numpy as jnp
from jax import lax
from jax.experimental import pallas as pl
from jax.experimental.pallas import tpu as pltpu
from jax.sharding import PartitionSpec as P

eps_norm = 1e-05
eps_mass = 1e-05
f32 = jnp.float32
bf16 = jnp.bfloat16
MIB = 1024 * 1024
FRONT_ROWS = 512
BACK_ROWS = 512


def dot(a, b):
    return jnp.dot(a, b, preferred_element_type=f32)


def dot_nt(a, b):
    return lax.dot_general(a, b, (((1,), (1,)), ((), ())), preferred_element_type=f32)


def split3(x):
    first = x.astype(bf16)
    rest = x - first.astype(f32)
    second = rest.astype(bf16)
    third = (rest - second.astype(f32)).astype(bf16)
    return first, second, third


def layer_norm(wide, gain):
    centered = wide - jnp.mean(wide, axis=-1, keepdims=True)
    variance = jnp.mean(centered * centered, axis=-1, keepdims=True)
    return (centered * lax.rsqrt(variance + eps_norm) * gain).astype(bf16)


def gelu(x):
    halved = 0.5 * x
    return halved + halved * lax.erf(x * math.sqrt(0.5))


def head_tile(weight, copies):
    size = weight.shape[0]
    wide = jnp.concatenate([weight] * copies, 1)
    tall = jnp.concatenate([wide] * copies, 0)
    row = lax.broadcasted_iota(jnp.int32, tall.shape, 0)
    col = lax.broadcasted_iota(jnp.int32, tall.shape, 1)
    return jnp.where(lax.div(row, size) == lax.div(col, size), tall, 0.0)


def front_kernel(
    zunit,
    sizes,
    place,
    gain,
    slice_weight,
    temp_vector,
    points,
    fx_weight,
    x_weight,
    stored,
    keep,
    send,
    fx_t,
    x_t,
    slice_t,
    temp_t,
    feats,
    mids,
    totals,
):
    head_size, slices = slice_weight.shape
    width = points.shape[1]
    heads = width // head_size
    quarter = heads // 4
    live = sizes[place[0]]
    core, turn = place[0] % 2, lax.div(place[0], zunit) % 2
    totals[...] = jnp.zeros_like(totals)
    slice_t[...] = slice_weight[...].astype(f32).T.astype(bf16)
    wide = jnp.concatenate([temp_vector[...]] * heads, 1)
    row = lax.broadcasted_iota(jnp.int32, (heads, width), 0)
    col = lax.broadcasted_iota(jnp.int32, (heads, width), 1)
    block = jnp.where(lax.div(col, head_size) == row, jnp.broadcast_to(wide, (heads, width)), 0.0)
    for i, part in enumerate(split3(block)):
        temp_t[i * heads : (i + 1) * heads, :] = part
    x_t[...] = x_weight[...].T
    fx_t[...] = fx_weight[...].T

    def own(h):
        return slice(h * head_size, (h + 1) * head_size)

    def add_sums(i, h):
        totals[h // quarter, own(h % quarter), :] += dot_nt(
            feats[own(h), :], stored[i, h * slices : (h + 1) * slices, :]
        )

    def step(i, carry):
        here = points[pl.ds(pl.multiple_of(i * FRONT_ROWS, FRONT_ROWS), FRONT_ROWS), :]
        normed = layer_norm(here.astype(f32), gain[...])
        mids[...] = dot_nt(x_t[...], normed).astype(bf16)
        feats[...] = dot_nt(fx_t[...], normed).astype(bf16)
        t = dot(temp_t[...], mids[...])
        t = t[:heads] + t[heads : 2 * heads] + t[2 * heads : 3 * heads]
        temps = 0.5 + jnp.maximum(t, 0.0) + jnp.log(1.0 + jnp.exp(-jnp.abs(t)))
        scales = math.log2(math.e) / temps
        col = lax.broadcasted_iota(jnp.int32, (1, FRONT_ROWS), 1) + i * FRONT_ROWS
        valid = jnp.where(col < live, 1.0, 0.0)
        for q in range(0, heads, 1):
            group = range(q, q + 1)
            logits = [dot(slice_t[...], mids[own(h), :]) for h in group]
            if q:
                for h in range(q - 1, q):
                    add_sums(i, h)
            tops = [jnp.max(l, axis=0, keepdims=True) for l in logits]
            raised = [
                jnp.exp2((l - top) * scales[h : h + 1, :]) for h, l, top in zip(group, logits, tops)
            ]
            shares = [valid * pltpu.reciprocal(jnp.sum(r, axis=0, keepdims=True), approx=True) for r in raised]
            for h, r, share in zip(group, raised, shares):
                weights = r * share
                stored[i, h * slices : (h + 1) * slices, :] = weights.astype(bf16)
                mass = weights[:, :128]
                for c in range(1, FRONT_ROWS // 128):
                    mass = mass + weights[:, c * 128 : (c + 1) * 128]
                mass_row = jnp.sum(mass.T, axis=0, keepdims=True)
                at = quarter * head_size + h % quarter
                totals[h // quarter, at : at + 1, :] += mass_row
        for h in range(heads - 1, heads):
            add_sums(i, h)
        return carry

    lax.fori_loop(0, lax.div(live + FRONT_ROWS - 1, FRONT_ROWS), step, 0)
    for n in range(2):
        keep[n] = totals[2 * core + (turn if n == 0 else 1 - turn)]
        send[n] = totals[2 * (1 - core) + (turn if n == 0 else 1 - turn)]


def mix_tokens(sums, crossed, value_t, repeat, tokens, queries, scores, probs, spread, at):
    slices = sums.shape[1]
    span = value_t.shape[0]
    half = scores.shape[0]
    head_size = span // half

    def own(h):
        return slice(h * head_size, (h + 1) * head_size)

    parts = []
    for h in range(half):
        mass = sums[span + h : span + h + 1, :] + eps_mass
        parts.append(sums[own(h), :] / mass)
    wide = jnp.concatenate(parts, 0)
    narrow = wide.astype(bf16)
    asked = dot(crossed[0], narrow) + dot(crossed[1], narrow) + dot(crossed[2], narrow)
    for i, part in enumerate(split3(asked * (math.log2(math.e) / math.sqrt(head_size)))):
        for h in range(half):
            queries[h, own(i), :] = part[own(h), :]
    values = dot(value_t[...], narrow).astype(bf16)
    tokens[...] = dot(narrow.T, repeat[...]).astype(bf16)
    for h in range(half):
        scores[h] = dot(tokens[:, h * 128 : (h + 1) * 128], queries[h])
    for h in range(half):
        top = jnp.max(scores[h], axis=0, keepdims=True)
        raised = jnp.exp2(scores[h] - top)
        total = jnp.sum(raised, axis=0, keepdims=True)
        probs[h] = (raised * pltpu.reciprocal(total, approx=True)).astype(bf16)
        if h:
            spread[at + (h - 1) * head_size : at + h * head_size, :] = dot(
                values[own(h - 1), :], probs[h - 1]
            ).astype(bf16)
    spread[at + span - head_size : at + span, :] = dot(values[own(half - 1), :], probs[half - 1]).astype(bf16)


def mix_weights(q_weight, k_weight, v_weight, crossed, value_t, repeat, queries):
    half, head_size = queries.shape[0], q_weight.shape[0]
    span = half * head_size
    tiled = head_tile(dot_nt(k_weight[...], q_weight[...]), half)
    for i, part in enumerate(split3(tiled)):
        crossed[i] = part
    value_t[...] = head_tile(v_weight[...].astype(f32), half).T.astype(bf16)
    row = lax.broadcasted_iota(jnp.int32, (span, half * 128), 0)
    col = lax.broadcasted_iota(jnp.int32, (span, half * 128), 1)
    same = (lax.div(row, head_size) == lax.div(col, 128)) & (
        lax.rem(row, head_size) == lax.rem(col, head_size)
    )
    repeat[...] = jnp.where(same, 1.0, 0.0).astype(bf16)
    queries[...] = jnp.zeros_like(queries)


def mix_kernel(sums, q_weight, k_weight, v_weight, out, crossed, value_t, repeat, tokens, queries, scores, probs):
    mix_weights(q_weight, k_weight, v_weight, crossed, value_t, repeat, queries)
    mix_tokens(sums, crossed, value_t, repeat, tokens, queries, scores, probs, out, 0)


def mix_scratch(half, head_size, slices):
    span = half * head_size
    return [
        pltpu.VMEM((3, span, span), bf16),
        pltpu.VMEM((span, span), bf16),
        pltpu.VMEM((span, half * 128), bf16),
        pltpu.VMEM((slices, half * 128), bf16),
        pltpu.VMEM((half, 128, slices), bf16),
        pltpu.VMEM((half, slices, slices), f32),
        pltpu.VMEM((half, slices, slices), bf16),
    ]


def back_kernel(
    zunit, sizes, place, stored, mine, across, along, corner, gain, points, out_weight, up, down, *refs
):
    extra = len(refs) - 5
    sent = refs[:extra]
    mixed, finished, spread, desliced, arrived = refs[extra:]
    span, slices = mine.shape
    rows, width = points.shape
    heads = stored.shape[1] // slices
    head_size = width // heads
    piece = up.shape[1] // 2
    live = sizes[place[0]]
    low = place[0] % 2 == 0
    near = lax.div(place[0], zunit) % 2 == 0
    blocks = rows // BACK_ROWS
    def leave(i):
        here = pl.ds(pl.multiple_of(i * BACK_ROWS, BACK_ROWS), BACK_ROWS)
        return pltpu.make_async_copy(finished.at[i], mixed.at[here, :], arrived.at[i])

    def own(h):
        return slice(h * head_size, (h + 1) * head_size)

    wide = [piece[...].astype(f32) for piece in (mine, across, along, corner)]
    for side in range(2):
        here = [jnp.where(low, wide[n + side], wide[n + 1 - side]) for n in (0, 2)]
        for part in range(2):
            at = (2 * side + part) * span
            spread[at : at + span, :] = jnp.where(near, here[part], here[1 - part]).astype(bf16)

    pieces = [
        (up.at[:, pl.ds(c * piece, piece)], down.at[pl.ds(c * piece, piece), :]) for c in range(2)
    ]
    if piece == width:
        pieces += [(r.at[pl.ds(0, width), :], r.at[pl.ds(width, piece), :]) for r in sent]
    else:
        pieces += [(sent[2 * i], sent[2 * i + 1]) for i in range(extra // 2)]

    def step(i, carry):
        per = BACK_ROWS // FRONT_ROWS
        for p in range(per):
            lanes = slice(p * FRONT_ROWS, (p + 1) * FRONT_ROWS)
            for h in range(heads):
                desliced[own(h), lanes] = dot(
                    spread[own(h), :], stored[i * per + p, h * slices : (h + 1) * slices, :]
                )
        picked = desliced[...].T.astype(bf16)
        here = points[pl.ds(pl.multiple_of(i * BACK_ROWS, BACK_ROWS), BACK_ROWS), :]
        residual = here.astype(f32) + dot(picked, out_weight[...])
        late = layer_norm(residual, gain[...])
        total = residual
        raw = dot(late, pieces[0][0][...])
        for n in range(len(pieces)):
            now = raw
            if n + 1 < len(pieces):
                raw = dot(late, pieces[n + 1][0][...])
            total = total + dot(gelu(now).astype(bf16), pieces[n][1][...])
        row = lax.broadcasted_iota(jnp.int32, (BACK_ROWS, 1), 0) + i * BACK_ROWS
        finished[i] = jnp.where(row < live, total, 0.0).astype(bf16)
        leave(i).start()
        return carry

    busy = lax.div(live + BACK_ROWS - 1, BACK_ROWS)
    lax.fori_loop(0, busy, step, 0)
    for i in range(blocks):

        @pl.when(i >= busy)
        def _():
            finished[i] = jnp.zeros_like(finished[i])
            leave(i).start()

    for i in range(blocks):
        leave(i).wait()


SMEM = pl.BlockSpec(memory_space=pltpu.SMEM)
VMEM = pl.BlockSpec(memory_space=pltpu.VMEM)
HBM = pl.BlockSpec(memory_space=pltpu.HBM)


def front_call(zunit, sizes, place, points, gain, fx_weight, x_weight, slice_weight, temp_vector):
    rows, width = points.shape
    head_size, slices = slice_weight.shape
    heads = width // head_size
    sums_rows = -(-(heads // 4 * (head_size + 1)) // 8) * 8
    return pl.pallas_call(
        functools.partial(front_kernel, zunit),
        in_specs=[SMEM, SMEM] + [VMEM] * 6,
        out_specs=[VMEM, VMEM, VMEM],
        out_shape=[
            jax.ShapeDtypeStruct((rows // FRONT_ROWS, heads * slices, FRONT_ROWS), bf16),
            jax.ShapeDtypeStruct((2, sums_rows, slices), f32),
            jax.ShapeDtypeStruct((2, sums_rows, slices), f32),
        ],
        scratch_shapes=[
            pltpu.VMEM((width, width), bf16),
            pltpu.VMEM((width, width), bf16),
            pltpu.VMEM((slices, head_size), bf16),
            pltpu.VMEM((3 * heads, width), bf16),
            pltpu.VMEM((width, FRONT_ROWS), bf16),
            pltpu.VMEM((width, FRONT_ROWS), bf16),
            pltpu.VMEM((4, sums_rows, slices), f32),
        ],
        compiler_params=pltpu.CompilerParams(vmem_limit_bytes=32 * MIB),
        name="front",
    )(
        sizes,
        place,
        gain[None, :],
        slice_weight,
        temp_vector[None, :],
        points,
        fx_weight,
        x_weight,
    )


def mix_call(sums, q_weight, k_weight, v_weight):
    head_size = q_weight.shape[0]
    slices = sums.shape[1]
    half = sums.shape[0] // (head_size + 1)
    return pl.pallas_call(
        mix_kernel,
        in_specs=[VMEM] * 4,
        out_specs=VMEM,
        out_shape=jax.ShapeDtypeStruct((half * head_size, slices), bf16),
        scratch_shapes=mix_scratch(half, head_size, slices),
        compiler_params=pltpu.CompilerParams(vmem_limit_bytes=12 * MIB),
        cost_estimate=pl.CostEstimate(flops=300_000_000, bytes_accessed=500_000, transcendentals=600_000),
        name="mix",
    )(sums, q_weight, k_weight, v_weight)


def back_call(zunit, sizes, place, stored, tokens, gain, points, out_weight, up, down, sent):
    rows, width = points.shape
    slices = tokens[0].shape[1]
    blocks = rows // BACK_ROWS
    return pl.pallas_call(
        functools.partial(back_kernel, zunit),
        in_specs=[SMEM, SMEM] + [VMEM] * (10 + len(sent)),
        out_specs=HBM,
        out_shape=jax.ShapeDtypeStruct((rows, width), bf16),
        scratch_shapes=[
            pltpu.VMEM((blocks, BACK_ROWS, width), bf16),
            pltpu.VMEM((width, slices), bf16),
            pltpu.VMEM((width, BACK_ROWS), f32),
            pltpu.SemaphoreType.DMA((blocks,)),
        ],
        compiler_params=pltpu.CompilerParams(vmem_limit_bytes=36 * MIB),
        name="back",
    )(
        sizes,
        place,
        stored,
        *tokens,
        gain[None, :],
        points,
        out_weight,
        up,
        down,
        *sent,
    )


def per_device(
    mesh_shape,
    points,
    part_sizes,
    norm1_gain,
    fx_weight,
    x_weight,
    slice_weight,
    temp_vector,
    q_weight,
    k_weight,
    v_weight,
    out_weight,
    norm2_gain,
    up_weight,
    down_weight,
):
    axes = ("pts", "ffn", "sub")
    devices = math.prod(mesh_shape[a] for a in axes)
    shards = mesh_shape["ffn"]
    place = lax.axis_index(axes).astype(jnp.int32).reshape(1)

    piece = up_weight.shape[1] // 2
    core = lax.axis_index("sub")
    halves = (
        lax.dynamic_slice_in_dim(up_weight, core * piece, piece, 1),
        lax.dynamic_slice_in_dim(down_weight, core * piece, piece, 0),
    )
    if piece == up_weight.shape[0]:
        halves = (jnp.concatenate(halves, 0),)
    far_pieces = [
        lax.ppermute(half, "ffn", [(i, (i + turn) % shards) for i in range(shards)])
        for turn in range(1, shards)
        for half in halves
    ]
    zunit = 2 * shards
    stored, keep, send = front_call(
        zunit, part_sizes, place, points, norm1_gain, fx_weight, x_weight, slice_weight, temp_vector
    )
    received = lax.ppermute(send, "sub", [(0, 1), (1, 0)])
    bits = [2 << b for b in range((devices // 2).bit_length() - 1)]
    zs = [b for b in bits if b > zunit]
    xs = [b for b in bits if b < zunit]

    def swap(x, even, odd):
        return lax.ppermute(x, axes, [(i, i ^ (odd if i & 1 else even)) for i in range(devices)])

    sums = keep[0] + received[0] + swap(keep[1] + received[1], zunit, zunit)
    for n, (even, odd) in enumerate(zip(zs + xs, xs + zs)):
        if n == len(zs + xs) - 1:
            ready = lax.optimization_barrier((tuple(far_pieces), sums))[0]
            hops = [lax.ppermute(piece, "sub", [(0, 1), (1, 0)]) for piece in ready]
        sums = sums + swap(sums, even, odd)
    mine = mix_call(sums, q_weight, k_weight, v_weight)
    along = swap(mine, zunit, zunit)
    pair = lax.ppermute(jnp.stack([mine, along]), "sub", [(0, 1), (1, 0)])
    tokens = [mine, pair[0], along, pair[1]]
    return back_call(
        zunit,
        part_sizes,
        place,
        stored,
        tokens,
        norm2_gain,
        points,
        out_weight,
        up_weight,
        down_weight,
        far_pieces + hops,
    )


def solution(mesh):
    return jax.shard_map(
        functools.partial(per_device, dict(mesh.shape)),
        mesh=mesh,
        in_specs=(
            P(("groups", "pts", "ffn", "sub"), None),
            P("groups"),
            P(),
            P(),
            P(),
            P(),
            P(),
            P(),
            P(),
            P(),
            P(),
            P(),
            P(None, "ffn"),
            P("ffn", None),
        ),
        out_specs=P(("groups", "pts", "ffn", "sub"), None),
        check_vma=False,
    )
```

```python
import functools
import math

import jax
import jax.numpy as jnp
from jax import lax
from jax.experimental import pallas as pl
from jax.experimental.pallas import tpu as pltpu
from jax.sharding import PartitionSpec as P

eps_norm = 1e-05
eps_mass = 1e-05
f32 = jnp.float32
bf16 = jnp.bfloat16
MIB = 1024 * 1024
FRONT_ROWS = 512
BACK_ROWS = 512


def dot(a, b):
    return jnp.dot(a, b, preferred_element_type=f32)


def dot_nt(a, b):
    return lax.dot_general(a, b, (((1,), (1,)), ((), ())), preferred_element_type=f32)


def split3(x):
    first = x.astype(bf16)
    rest = x - first.astype(f32)
    second = rest.astype(bf16)
    third = (rest - second.astype(f32)).astype(bf16)
    return first, second, third


def layer_norm(wide, gain):
    centered = wide - jnp.mean(wide, axis=-1, keepdims=True)
    variance = jnp.mean(centered * centered, axis=-1, keepdims=True)
    return (centered * lax.rsqrt(variance + eps_norm) * gain).astype(bf16)


def gelu(x):
    halved = 0.5 * x
    return halved + halved * lax.erf(x * math.sqrt(0.5))


def head_tile(weight, copies):
    size = weight.shape[0]
    wide = jnp.concatenate([weight] * copies, 1)
    tall = jnp.concatenate([wide] * copies, 0)
    row = lax.broadcasted_iota(jnp.int32, tall.shape, 0)
    col = lax.broadcasted_iota(jnp.int32, tall.shape, 1)
    return jnp.where(lax.div(row, size) == lax.div(col, size), tall, 0.0)


def front_kernel(
    zunit,
    sizes,
    place,
    gain,
    slice_weight,
    temp_vector,
    points,
    fx_weight,
    x_weight,
    stored,
    keep,
    send,
    fx_t,
    x_t,
    slice_t,
    temp_t,
    feats,
    mids,
    totals,
):
    head_size, slices = slice_weight.shape
    width = points.shape[1]
    heads = width // head_size
    quarter = heads // 4
    live = sizes[place[0]]
    core, turn = place[0] % 2, lax.div(place[0], zunit) % 2
    totals[...] = jnp.zeros_like(totals)
    slice_t[...] = slice_weight[...].astype(f32).T.astype(bf16)
    wide = jnp.concatenate([temp_vector[...]] * heads, 1)
    row = lax.broadcasted_iota(jnp.int32, (heads, width), 0)
    col = lax.broadcasted_iota(jnp.int32, (heads, width), 1)
    block = jnp.where(lax.div(col, head_size) == row, jnp.broadcast_to(wide, (heads, width)), 0.0)
    for i, part in enumerate(split3(block)):
        temp_t[i * heads : (i + 1) * heads, :] = part
    x_t[...] = x_weight[...].astype(f32).T.astype(bf16)
    fx_t[...] = fx_weight[...].astype(f32).T.astype(bf16)

    def own(h):
        return slice(h * head_size, (h + 1) * head_size)

    def add_sums(i, h):
        totals[h // quarter, own(h % quarter), :] += dot_nt(
            feats[own(h), :], stored[i, h * slices : (h + 1) * slices, :]
        )

    def step(i, carry):
        here = points[pl.ds(pl.multiple_of(i * FRONT_ROWS, FRONT_ROWS), FRONT_ROWS), :]
        normed = layer_norm(here.astype(f32), gain[...])
        mids[...] = dot_nt(x_t[...], normed).astype(bf16)
        feats[...] = dot_nt(fx_t[...], normed).astype(bf16)
        t = dot(temp_t[...], mids[...])
        t = t[:heads] + t[heads : 2 * heads] + t[2 * heads : 3 * heads]
        temps = 0.5 + jnp.maximum(t, 0.0) + jnp.log(1.0 + jnp.exp(-jnp.abs(t)))
        scales = math.log2(math.e) / temps
        col = lax.broadcasted_iota(jnp.int32, (1, FRONT_ROWS), 1) + i * FRONT_ROWS
        valid = jnp.where(col < live, 1.0, 0.0)
        for q in range(0, heads, 1):
            group = range(q, q + 1)
            logits = [dot(slice_t[...], mids[own(h), :]) for h in group]
            if q:
                for h in range(q - 1, q):
                    add_sums(i, h)
            tops = [jnp.max(l, axis=0, keepdims=True) for l in logits]
            raised = [
                jnp.exp2((l - top) * scales[h : h + 1, :]) for h, l, top in zip(group, logits, tops)
            ]
            shares = [valid * pltpu.reciprocal(jnp.sum(r, axis=0, keepdims=True), approx=True) for r in raised]
            for h, r, share in zip(group, raised, shares):
                weights = r * share
                stored[i, h * slices : (h + 1) * slices, :] = weights.astype(bf16)
                mass = weights[:, :128]
                for c in range(1, FRONT_ROWS // 128):
                    mass = mass + weights[:, c * 128 : (c + 1) * 128]
                mass_row = jnp.sum(mass.T, axis=0, keepdims=True)
                at = quarter * head_size + h % quarter
                totals[h // quarter, at : at + 1, :] += mass_row
        for h in range(heads - 1, heads):
            add_sums(i, h)
        return carry

    lax.fori_loop(0, lax.div(live + FRONT_ROWS - 1, FRONT_ROWS), step, 0)
    for n in range(2):
        keep[n] = totals[2 * core + (turn if n == 0 else 1 - turn)]
        send[n] = totals[2 * (1 - core) + (turn if n == 0 else 1 - turn)]


def mix_tokens(sums, crossed, value_t, repeat, tokens, queries, scores, probs, spread, at):
    slices = sums.shape[1]
    span = value_t.shape[0]
    half = scores.shape[0]
    head_size = span // half

    def own(h):
        return slice(h * head_size, (h + 1) * head_size)

    parts = []
    for h in range(half):
        mass = sums[span + h : span + h + 1, :] + eps_mass
        parts.append(sums[own(h), :] / mass)
    wide = jnp.concatenate(parts, 0)
    narrow = wide.astype(bf16)
    asked = dot(crossed[0], narrow) + dot(crossed[1], narrow) + dot(crossed[2], narrow)
    for i, part in enumerate(split3(asked * (math.log2(math.e) / math.sqrt(head_size)))):
        for h in range(half):
            queries[h, own(i), :] = part[own(h), :]
    values = dot(value_t[...], narrow).astype(bf16)
    tokens[...] = dot(narrow.astype(f32).T.astype(bf16), repeat[...]).astype(bf16)
    for h in range(half):
        scores[h] = dot(tokens[:, h * 128 : (h + 1) * 128], queries[h])
    for h in range(half):
        top = jnp.max(scores[h], axis=0, keepdims=True)
        raised = jnp.exp2(scores[h] - top)
        total = jnp.sum(raised, axis=0, keepdims=True)
        probs[h] = (raised * pltpu.reciprocal(total, approx=True)).astype(bf16)
        if h:
            spread[at + (h - 1) * head_size : at + h * head_size, :] = dot(
                values[own(h - 1), :], probs[h - 1]
            ).astype(bf16)
    spread[at + span - head_size : at + span, :] = dot(values[own(half - 1), :], probs[half - 1]).astype(bf16)


def mix_weights(q_weight, k_weight, v_weight, crossed, value_t, repeat, queries):
    half, head_size = queries.shape[0], q_weight.shape[0]
    span = half * head_size
    tiled = head_tile(dot_nt(k_weight[...], q_weight[...]), half)
    for i, part in enumerate(split3(tiled)):
        crossed[i] = part
    value_t[...] = head_tile(v_weight[...].astype(f32), half).T.astype(bf16)
    row = lax.broadcasted_iota(jnp.int32, (span, half * 128), 0)
    col = lax.broadcasted_iota(jnp.int32, (span, half * 128), 1)
    same = (lax.div(row, head_size) == lax.div(col, 128)) & (
        lax.rem(row, head_size) == lax.rem(col, head_size)
    )
    repeat[...] = jnp.where(same, 1.0, 0.0).astype(bf16)
    queries[...] = jnp.zeros_like(queries)


def mix_kernel(sums, q_weight, k_weight, v_weight, out, crossed, value_t, repeat, tokens, queries, scores, probs):
    mix_weights(q_weight, k_weight, v_weight, crossed, value_t, repeat, queries)
    mix_tokens(sums, crossed, value_t, repeat, tokens, queries, scores, probs, out, 0)


def mix_scratch(half, head_size, slices):
    span = half * head_size
    return [
        pltpu.VMEM((3, span, span), bf16),
        pltpu.VMEM((span, span), bf16),
        pltpu.VMEM((span, half * 128), bf16),
        pltpu.VMEM((slices, half * 128), bf16),
        pltpu.VMEM((half, 128, slices), bf16),
        pltpu.VMEM((half, slices, slices), f32),
        pltpu.VMEM((half, slices, slices), bf16),
    ]


def back_kernel(
    zunit, sizes, place, stored, mine, across, along, corner, gain, points, out_weight, up, down, *refs
):
    extra = len(refs) - 5
    sent = refs[:extra]
    mixed, finished, spread, desliced, arrived = refs[extra:]
    span, slices = mine.shape
    rows, width = points.shape
    heads = stored.shape[1] // slices
    head_size = width // heads
    piece = up.shape[1] // 2
    live = sizes[place[0]]
    low = place[0] % 2 == 0
    near = lax.div(place[0], zunit) % 2 == 0
    blocks = rows // BACK_ROWS
    def leave(i):
        here = pl.ds(pl.multiple_of(i * BACK_ROWS, BACK_ROWS), BACK_ROWS)
        return pltpu.make_async_copy(finished.at[i], mixed.at[here, :], arrived.at[i])

    def own(h):
        return slice(h * head_size, (h + 1) * head_size)

    wide = [piece[...].astype(f32) for piece in (mine, across, along, corner)]
    for side in range(2):
        here = [jnp.where(low, wide[n + side], wide[n + 1 - side]) for n in (0, 2)]
        for part in range(2):
            at = (2 * side + part) * span
            spread[at : at + span, :] = jnp.where(near, here[part], here[1 - part]).astype(bf16)

    pieces = [
        (up.at[:, pl.ds(c * piece, piece)], down.at[pl.ds(c * piece, piece), :]) for c in range(2)
    ]
    if piece == width:
        pieces += [(r.at[pl.ds(0, width), :], r.at[pl.ds(width, piece), :]) for r in sent]
    else:
        pieces += [(sent[2 * i], sent[2 * i + 1]) for i in range(extra // 2)]

    def step(i, carry):
        per = BACK_ROWS // FRONT_ROWS
        for p in range(per):
            lanes = slice(p * FRONT_ROWS, (p + 1) * FRONT_ROWS)
            for h in range(heads):
                desliced[own(h), lanes] = dot(
                    spread[own(h), :], stored[i * per + p, h * slices : (h + 1) * slices, :]
                )
        picked = desliced[...].T.astype(bf16)
        here = points[pl.ds(pl.multiple_of(i * BACK_ROWS, BACK_ROWS), BACK_ROWS), :]
        residual = here.astype(f32) + dot(picked, out_weight[...])
        late = layer_norm(residual, gain[...])
        total = residual
        raw = dot(late, pieces[0][0][...])
        for n in range(len(pieces)):
            now = raw
            if n + 1 < len(pieces):
                raw = dot(late, pieces[n + 1][0][...])
            total = total + dot(gelu(now).astype(bf16), pieces[n][1][...])
        row = lax.broadcasted_iota(jnp.int32, (BACK_ROWS, 1), 0) + i * BACK_ROWS
        finished[i] = jnp.where(row < live, total, 0.0).astype(bf16)
        leave(i).start()
        return carry

    busy = lax.div(live + BACK_ROWS - 1, BACK_ROWS)
    lax.fori_loop(0, busy, step, 0)
    for i in range(blocks):

        @pl.when(i >= busy)
        def _():
            finished[i] = jnp.zeros_like(finished[i])
            leave(i).start()

    for i in range(blocks):
        leave(i).wait()


SMEM = pl.BlockSpec(memory_space=pltpu.SMEM)
VMEM = pl.BlockSpec(memory_space=pltpu.VMEM)
HBM = pl.BlockSpec(memory_space=pltpu.HBM)


def front_call(zunit, sizes, place, points, gain, fx_weight, x_weight, slice_weight, temp_vector):
    rows, width = points.shape
    head_size, slices = slice_weight.shape
    heads = width // head_size
    sums_rows = -(-(heads // 4 * (head_size + 1)) // 8) * 8
    return pl.pallas_call(
        functools.partial(front_kernel, zunit),
        in_specs=[SMEM, SMEM] + [VMEM] * 6,
        out_specs=[VMEM, VMEM, VMEM],
        out_shape=[
            jax.ShapeDtypeStruct((rows // FRONT_ROWS, heads * slices, FRONT_ROWS), bf16),
            jax.ShapeDtypeStruct((2, sums_rows, slices), f32),
            jax.ShapeDtypeStruct((2, sums_rows, slices), f32),
        ],
        scratch_shapes=[
            pltpu.VMEM((width, width), bf16),
            pltpu.VMEM((width, width), bf16),
            pltpu.VMEM((slices, head_size), bf16),
            pltpu.VMEM((3 * heads, width), bf16),
            pltpu.VMEM((width, FRONT_ROWS), bf16),
            pltpu.VMEM((width, FRONT_ROWS), bf16),
            pltpu.VMEM((4, sums_rows, slices), f32),
        ],
        compiler_params=pltpu.CompilerParams(vmem_limit_bytes=32 * MIB),
        name="front",
    )(
        sizes,
        place,
        gain[None, :],
        slice_weight,
        temp_vector[None, :],
        points,
        fx_weight,
        x_weight,
    )


def mix_call(sums, q_weight, k_weight, v_weight):
    head_size = q_weight.shape[0]
    slices = sums.shape[1]
    half = sums.shape[0] // (head_size + 1)
    return pl.pallas_call(
        mix_kernel,
        in_specs=[VMEM] * 4,
        out_specs=VMEM,
        out_shape=jax.ShapeDtypeStruct((half * head_size, slices), bf16),
        scratch_shapes=mix_scratch(half, head_size, slices),
        compiler_params=pltpu.CompilerParams(vmem_limit_bytes=12 * MIB),
        cost_estimate=pl.CostEstimate(flops=300_000_000, bytes_accessed=500_000, transcendentals=600_000),
        name="mix",
    )(sums, q_weight, k_weight, v_weight)


def back_call(zunit, sizes, place, stored, tokens, gain, points, out_weight, up, down, sent):
    rows, width = points.shape
    slices = tokens[0].shape[1]
    blocks = rows // BACK_ROWS
    return pl.pallas_call(
        functools.partial(back_kernel, zunit),
        in_specs=[SMEM, SMEM] + [VMEM] * (10 + len(sent)),
        out_specs=HBM,
        out_shape=jax.ShapeDtypeStruct((rows, width), bf16),
        scratch_shapes=[
            pltpu.VMEM((blocks, BACK_ROWS, width), bf16),
            pltpu.VMEM((width, slices), bf16),
            pltpu.VMEM((width, BACK_ROWS), f32),
            pltpu.SemaphoreType.DMA((blocks,)),
        ],
        compiler_params=pltpu.CompilerParams(vmem_limit_bytes=36 * MIB),
        name="back",
    )(
        sizes,
        place,
        stored,
        *tokens,
        gain[None, :],
        points,
        out_weight,
        up,
        down,
        *sent,
    )


def per_device(
    mesh_shape,
    points,
    part_sizes,
    norm1_gain,
    fx_weight,
    x_weight,
    slice_weight,
    temp_vector,
    q_weight,
    k_weight,
    v_weight,
    out_weight,
    norm2_gain,
    up_weight,
    down_weight,
):
    axes = ("pts", "ffn", "sub")
    devices = math.prod(mesh_shape[a] for a in axes)
    shards = mesh_shape["ffn"]
    place = lax.axis_index(axes).astype(jnp.int32).reshape(1)

    piece = up_weight.shape[1] // 2
    core = lax.axis_index("sub")
    halves = (
        lax.dynamic_slice_in_dim(up_weight, core * piece, piece, 1),
        lax.dynamic_slice_in_dim(down_weight, core * piece, piece, 0),
    )
    if piece == up_weight.shape[0]:
        halves = (jnp.concatenate(halves, 0),)
    far_pieces = [
        lax.ppermute(half, "ffn", [(i, (i + turn) % shards) for i in range(shards)])
        for turn in range(1, shards)
        for half in halves
    ]
    zunit = 2 * shards
    stored, keep, send = front_call(
        zunit, part_sizes, place, points, norm1_gain, fx_weight, x_weight, slice_weight, temp_vector
    )
    received = lax.ppermute(send, "sub", [(0, 1), (1, 0)])
    bits = [2 << b for b in range((devices // 2).bit_length() - 1)]
    zs = [b for b in bits if b > zunit]
    xs = [b for b in bits if b < zunit]

    def swap(x, even, odd):
        return lax.ppermute(x, axes, [(i, i ^ (odd if i & 1 else even)) for i in range(devices)])

    sums = keep[0] + received[0] + swap(keep[1] + received[1], zunit, zunit)
    for n, (even, odd) in enumerate(zip(zs + xs, xs + zs)):
        if n == len(zs + xs) - 1:
            ready = lax.optimization_barrier((tuple(far_pieces), sums))[0]
            hops = [lax.ppermute(piece, "sub", [(0, 1), (1, 0)]) for piece in ready]
        sums = sums + swap(sums, even, odd)
    mine = mix_call(sums, q_weight, k_weight, v_weight)
    across, along = swap(mine, 1, 1), swap(mine, zunit, zunit)
    tokens = [mine, across, along, swap(along, 1, 1)]
    return back_call(
        zunit,
        part_sizes,
        place,
        stored,
        tokens,
        norm2_gain,
        points,
        out_weight,
        up_weight,
        down_weight,
        far_pieces + hops,
    )


def solution(mesh):
    return jax.shard_map(
        functools.partial(per_device, dict(mesh.shape)),
        mesh=mesh,
        in_specs=(
            P(("groups", "pts", "ffn", "sub"), None),
            P("groups"),
            P(),
            P(),
            P(),
            P(),
            P(),
            P(),
            P(),
            P(),
            P(),
            P(),
            P(None, "ffn"),
            P("ffn", None),
        ),
        out_specs=P(("groups", "pts", "ffn", "sub"), None),
        check_vma=False,
    )
```
